32 devices in a mesh: groups: 2 (over y), devs: 8 (over z, x), pair: 2 (over core).
Axes of the slice: x: 2, y: 2, z: 4, core: 2. Of those that a mesh axis runs over, the one named last changes fastest.
Arguments:
- query: bfloat16 [2, 64, 3072], P(None, ('groups', 'devs'), 'pair'), parts along dimension 1, may hold values from -66 to 66
- key_cache: bfloat16 [2, 64, 256, 512], P(None, ('groups', 'devs'), None, 'pair'), parts along dimension 1, may hold values from -7 to 7
- value_cache: bfloat16 [2, 64, 256, 512], P(None, ('groups', 'devs'), None, 'pair'), parts along dimension 1, may hold values from -18 to 18
- lengths: int32 [2, 64], P(None, ('groups', 'devs')), parts along dimension 1, may hold values from 2 to 256, as said below
- residual: bfloat16 [2, 64, 3072], P(None, ('groups', 'devs'), 'pair'), parts along dimension 1, may hold values from -180 to 180
- router: bfloat16 [3072, 4], P('pair'), may hold values from -0.109375 to 0.109375
- routes: int32 [2, 64, 2], P(None, ('groups', 'devs')), parts along dimension 1, may hold values from 0 to 3, all different within a row; in each aligned block of 4 rows (0 to 3, 4 to 7, ..., all dimensions but the last counted through in order) at most 3 rows name the same one
- w_gate: bfloat16 [3072, 32768], P(None, ('devs', 'pair')), may hold values from -0.109375 to 0.109375
- w_up: bfloat16 [3072, 32768], P(None, ('devs', 'pair')), may hold values from -0.109375 to 0.109375
- w_down: bfloat16 [32768, 3072], P(('devs', 'pair')), may hold values from -0.0625 to 0.0625
Outputs:
- mixed: bfloat16 [2, 64, 3072], P(None, ('groups', 'devs'), 'pair'), parts along dimension 1
The draws below stay inside these ranges and needn't reach their ends.
There are 2 independent parts, one for each index of `groups`. The reference program is written for one: setup_inputs(seed, part) draws one part's arguments, and reference() takes and returns one part's arrays. A program takes and returns all parts, laid end to end along the dimension named above; an argument that names none is the same for every part. Nothing has to cross between parts.
Inputs may be any that keep to these rules, and one draw needn't show every extreme that they name: `lengths`: at least one request of each draw has all 256 entries live. `routes`: among the requests of one index of devs in one micro-batch no expert is named more than 3 times, a bound that some such block reaches.
All inputs are finite; a program needn't handle non-finite values.
Results may differ from the reference program's by a relative error of at most 0.0056.
Values may be sent and summed in bfloat16 or wider, within the bound.
No kernel may reach another device: no remote copies, remote signals or barrier semaphores. Data moves between devices by JAX's collectives and lax.ppermute only.
A program may use at most 128 MiB of HBM per device.

```python
import math
import jax
import jax.numpy as jnp
import numpy as np
from jax import lax

D = 3072
H = 24
KVH = 4
HD = 128
EXPERTS = 4
FF = 8192
MB = 2
RQ_DEV = 4
CACHE = 256
CAP = 3
REQS = 32


def draw_query(key, part):
    key = jax.random.fold_in(key, 11)
    noise_key = jax.random.fold_in(key, 0)
    base = jnp.clip(jax.random.normal(noise_key, (MB, REQS, H, HD), jnp.float32), -6.0, 6.0)
    return base.reshape(MB, REQS, H * HD).astype(jnp.bfloat16)


def draw_key_cache(key, part):
    key = jax.random.fold_in(key, 12)
    base = jnp.clip(jax.random.normal(key, (MB, REQS, CACHE, KVH, HD), jnp.float32), -6.0, 6.0)
    return base.reshape(MB, REQS, CACHE, KVH * HD).astype(jnp.bfloat16)


def draw_residual(key, part):
    key = jax.random.fold_in(key, 13)
    noise_key = jax.random.fold_in(key, 0)
    base = jnp.clip(jax.random.normal(noise_key, (MB, REQS, D), jnp.float32), -6.0, 6.0)
    return base.astype(jnp.bfloat16)


def draw_lengths(key, part):
    key = jax.random.fold_in(key, 14)
    length_key, index_key = jax.random.split(key)
    drawn = jax.random.randint(length_key, (MB * REQS,), 2, CACHE + 1, dtype=jnp.int32)
    fullest = jax.random.randint(index_key, (), 0, MB * REQS, dtype=jnp.int32)
    drawn = jnp.where(jnp.arange(MB * REQS, dtype=jnp.int32) == fullest, CACHE, drawn)
    return drawn.reshape(MB, REQS)


def shard_levels(own_key, shape, pieces, least, top_value):
    factor_of = 1.0
    for dim, parts in pieces:
        steps = jax.random.uniform(jax.random.fold_in(jax.random.fold_in(own_key, 6), dim), (parts,), jnp.float32, least / len(pieces), top_value / len(pieces))
        factor_of = factor_of * jnp.repeat(jnp.exp(steps), shape[dim] // parts).reshape((-1,) + (1,) * (len(shape) - 1 - dim))
    return factor_of


def assign_block(key, own, number, rows, number_of, top, reach, lean):
    ranking = jax.random.permutation(key, number_of)
    crowded, ordinary = portions_of(number_of, rows * top, reach, lean, True), portions_of(number_of, rows * top, reach, lean, False)
    places = jnp.arange(number_of)

    def named(sizes, offset_by):
        used = int((sizes > 0).sum())
        fixed = max(1, used // 4)
        shifted = fixed + (places - fixed + offset_by * (used - fixed)) % max(1, number_of - fixed)
        return jnp.zeros((number_of,), jnp.int32).at[ranking[jnp.where(places < fixed, places, shifted)]].set(jnp.asarray(sizes, jnp.int32))

    sizes = jnp.where(number % 4 == 0, named(crowded, number // 4), named(ordinary, number - number // 4 - 1))
    mixed = jax.random.permutation(jax.random.fold_in(own, 3), number_of)
    source_of, receiver = mixed[0:number_of // 2 * 2:2], mixed[1:number_of // 2 * 2:2]
    margin = jnp.minimum(sizes[source_of] - 1, reach - sizes[receiver]) // 2
    margin = jnp.where((source_of == ranking[0]) | (receiver == ranking[0]) | (sizes[receiver] == 0), 0, jnp.maximum(margin, 0))
    shifted = jax.random.randint(jax.random.fold_in(own, 4), (number_of // 2,), 0, 1 << 20) % (margin + 1)
    sizes = sizes.at[source_of].add(-shifted).at[receiver].add(shifted)
    labels = jnp.searchsorted(jnp.cumsum(sizes), jnp.arange(rows * top), side="right").astype(jnp.int32)
    listing = labels.reshape(top, rows).T
    listing = listing[jax.random.permutation(jax.random.fold_in(own, 1), rows)]
    offset_by = jax.random.randint(jax.random.fold_in(own, 2), (rows, 1), 0, top)
    return jnp.take_along_axis(listing, (jnp.arange(top)[None, :] + offset_by) % top, axis=1)


def portions_of(count, total, limit, lean, full):
    portions = [(1 << 20) // math.isqrt(standing ** lean) + 1 for standing in range(1, count + 1)]
    largest = limit if full else min(limit, max(-(-total // count), total * portions[0] // sum(portions)))
    least = 1 if total - largest >= count - 1 else 0
    given, surplus = [largest] + [least] * (count - 1), total - largest - least * (count - 1)
    while surplus > 0:
        movable = [i for i in range(1, count) if given[i] < largest] or [i for i in range(1, count) if given[i] < limit]
        whole, remaining = sum([portions[i] for i in movable]), surplus
        for i in movable:
            addition = min(limit - given[i], max(1, remaining * portions[i] // whole), surplus)
            given[i] = given[i] + addition
            surplus = surplus - addition
    return np.array(given)


def gaussian(key, dims, width, limit, cuts=(), held_as=jnp.bfloat16):
    values = jax.random.normal(key, dims, jnp.float32) * width
    if len(cuts) > 0:
        values = shard_levels(key, dims, cuts, -0.22, 0.18) * values
    return jnp.clip(values, min=-limit, max=limit).astype(held_as)


def setup_inputs(seed: int = 0, part: int = 0) -> dict:
    seeds = jax.random.split(jax.random.key(seed), 11)
    part_keys = jax.random.split(jax.random.fold_in(seeds[10], part), 11)
    query = draw_query(jax.random.fold_in(jax.random.fold_in(seeds[10], part), 71), part)
    key_cache = draw_key_cache(jax.random.fold_in(jax.random.fold_in(seeds[10], part), 71), part)
    value_cache = gaussian(part_keys[2], (MB, REQS, CACHE, KVH * HD), 3.0, 18.0, ((1, 8), (3, 2)))
    lengths = draw_lengths(jax.random.fold_in(jax.random.fold_in(seeds[10], part), 71), part)
    residual = draw_residual(jax.random.fold_in(jax.random.fold_in(seeds[10], part), 71), part)
    router = gaussian(seeds[5], (D, EXPERTS), D ** -0.5, 0.109375, ((0, 2),))
    routes_keys = jax.random.split(jax.random.fold_in(part_keys[6], 1), MB * REQS // RQ_DEV)
    routes_turns = jax.random.permutation(jax.random.fold_in(part_keys[6], 3), MB * REQS // RQ_DEV)
    routes = jax.vmap(lambda own, number: assign_block(jax.random.fold_in(part_keys[6], 2), own, number, RQ_DEV, EXPERTS, 2, CAP, 2))(routes_keys, routes_turns).reshape((MB, REQS, 2))
    w_gate = gaussian(seeds[7], (D, EXPERTS * FF), D ** -0.5, 0.109375, ((1, 16),))
    w_up = gaussian(seeds[8], (D, EXPERTS * FF), D ** -0.5, 0.109375, ((1, 16),))
    w_down = gaussian(seeds[9], (EXPERTS * FF, D), FF ** -0.5, 0.0625, ((0, 16),))
    return dict(query=query, key_cache=key_cache, value_cache=value_cache, lengths=lengths, residual=residual, router=router, routes=routes, w_gate=w_gate, w_up=w_up, w_down=w_down)


def attend(query, key_cache, value_cache, lengths):
    group_size = H // KVH
    queries = query.astype(jnp.float32).reshape(REQS, KVH, group_size, HD)
    keys_all = key_cache.astype(jnp.float32).reshape(REQS, CACHE, KVH, HD)
    values_all = value_cache.astype(jnp.float32).reshape(REQS, CACHE, KVH, HD)
    scores = jnp.einsum('rkgd,rtkd->rkgt', queries, keys_all) * (1.0 / math.sqrt(HD))
    live_mask = (jnp.arange(CACHE, dtype=jnp.int32)[None, :] < lengths[:, None])[:, None, None, :]
    scores = jnp.where(live_mask, scores, -jnp.inf)
    peak_score = lax.optimization_barrier(jnp.max(scores, axis=-1, keepdims=True))
    weights_exp = jnp.where(live_mask, jnp.exp(scores - peak_score), 0.0)
    total_weight = lax.optimization_barrier(jnp.sum(weights_exp, axis=-1, keepdims=True))
    rounded = lax.optimization_barrier(weights_exp.astype(jnp.bfloat16)).astype(jnp.float32)
    mixed_heads = jnp.einsum('rkgt,rtkd->rkgd', rounded, values_all) / total_weight
    return mixed_heads.reshape(REQS, D)

def reference(query, key_cache, value_cache, lengths, residual, router, routes, w_gate, w_up, w_down):
    outputs = []
    for batch_index in range(MB):
        attended = attend(query[batch_index], key_cache[batch_index], value_cache[batch_index], lengths[batch_index])
        hidden = lax.optimization_barrier((residual[batch_index].astype(jnp.float32) + attended).astype(jnp.bfloat16))
        hidden_wide = hidden.astype(jnp.float32)
        inv_rms = lax.rsqrt(lax.optimization_barrier(jnp.mean(hidden_wide * hidden_wide, axis=-1, keepdims=True)) + 1e-05)
        normed = (hidden_wide * inv_rms).astype(jnp.bfloat16)
        logits = jnp.dot(hidden, router, preferred_element_type=jnp.float32) * inv_rms
        chosen = routes[batch_index]
        logit_first = jnp.take_along_axis(logits, chosen[:, 0:1], axis=1)[:, 0]
        logit_second = jnp.take_along_axis(logits, chosen[:, 1:2], axis=1)[:, 0]
        gate_first = jax.nn.sigmoid(logit_first - logit_second)
        gate_second = jax.nn.sigmoid(logit_second - logit_first)
        result = hidden_wide
        for expert in range(EXPERTS):
            column_start = expert * FF
            gate_proj = jnp.dot(normed, w_gate[:, column_start:column_start + FF], preferred_element_type=jnp.float32)
            up_proj = jnp.dot(normed, w_up[:, column_start:column_start + FF], preferred_element_type=jnp.float32)
            hidden_units = (jax.nn.silu(gate_proj) * up_proj).astype(jnp.bfloat16)
            expert_out = jnp.dot(hidden_units, w_down[column_start:column_start + FF], preferred_element_type=jnp.float32)
            weight = jnp.where(chosen[:, 0] == expert, gate_first, 0.0) + jnp.where(chosen[:, 1] == expert, gate_second, 0.0)
            result = result + weight[:, None] * expert_out
        outputs.append(result.astype(jnp.bfloat16))
    return jnp.stack(outputs)
```

```python
import functools
import math

import jax
import jax.numpy as jnp
from jax import lax
from jax.experimental import pallas as pl
from jax.experimental.pallas import tpu as pltpu
from jax.sharding import PartitionSpec as P

HD = 128
LANES = 128


def attend_kernel(
    query_ref, key_ref, value_ref, lengths_ref, residual_ref, router_ref, outgoing_ref, meta_ref
):
    batches, per_batch, width = query_ref.shape
    rows = batches * per_batch
    cache_len = key_ref.shape[2]
    kv_local = key_ref.shape[3] // HD
    group = width // key_ref.shape[3]

    def stacked(ref):
        return jnp.concatenate([ref[b].astype(jnp.float32) for b in range(batches)], axis=0)

    queries = stacked(query_ref)
    residual = stacked(residual_ref)
    tall = group * rows
    row_of = lax.rem(lax.broadcasted_iota(jnp.int32, (tall, 1), 0), rows)
    position = lax.broadcasted_iota(jnp.int32, (tall, cache_len), 1)
    limit = jnp.zeros((tall, 1), jnp.int32)
    for r in range(rows):
        limit = jnp.where(row_of == r, lengths_ref[r // per_batch, r % per_batch], limit)
    live = position < limit
    pieces = []
    for k in range(kv_local):
        heads = jnp.concatenate(
            [queries[:, (k * group + j) * HD : (k * group + j + 1) * HD] for j in range(group)],
            axis=0,
        ).astype(jnp.bfloat16)
        columns = slice(k * HD, (k + 1) * HD)
        scores = jnp.zeros((tall, cache_len), jnp.float32)
        for r in range(rows):
            keys = key_ref[r // per_batch, r % per_batch, :, columns]
            part = lax.dot_general(
                heads, keys, (((1,), (1,)), ((), ())), preferred_element_type=jnp.float32
            )
            scores = jnp.where(row_of == r, part, scores)
        scores = jnp.where(live, scores * (1.0 / math.sqrt(HD)), -jnp.inf)
        peak = jnp.max(scores, axis=-1, keepdims=True)
        weights = jnp.where(live, jnp.exp(scores - peak), 0.0)
        total = jnp.sum(weights, axis=-1, keepdims=True)
        weights_bf = weights.astype(jnp.bfloat16)
        mixed = jnp.zeros((tall, HD), jnp.float32)
        for r in range(rows):
            values = value_ref[r // per_batch, r % per_batch, :, columns]
            part = jnp.dot(weights_bf, values, preferred_element_type=jnp.float32)
            mixed = jnp.where(row_of == r, part, mixed)
        mixed = mixed / total
        pieces += [mixed[j * rows : (j + 1) * rows] for j in range(group)]
    attended = jnp.concatenate(pieces, axis=1)
    hidden = (residual + attended).astype(jnp.bfloat16)
    wide = hidden.astype(jnp.float32)
    logits = jnp.dot(hidden, router_ref[...], preferred_element_type=jnp.float32)
    squares = jnp.sum(wide * wide, axis=-1, keepdims=True)
    experts = router_ref.shape[1]
    meta_ref[...] = jnp.zeros_like(meta_ref)
    meta_ref[:, :experts] = logits
    meta_ref[:, experts : experts + 1] = squares
    for d in range(outgoing_ref.shape[0]):
        outgoing_ref[d] = hidden


def expert_kernel(
    side_ref, own_ref, other_ref, gate_ref, up_ref, down_ref, kept_ref, sent_ref, normed, total
):
    step = pl.program_id(0)
    half = own_ref.shape[-1]
    side = side_ref[0]
    own_columns = pl.ds(pl.multiple_of(side * half, LANES), half)
    other_columns = pl.ds(pl.multiple_of((1 - side) * half, LANES), half)
    count = normed.shape[0]

    @pl.when(step == 0)
    def _():
        own = own_ref[...].astype(jnp.float32).reshape(count, half)
        other = other_ref[...].astype(jnp.float32).reshape(count, half)
        squares = jnp.sum(own * own, axis=-1, keepdims=True) + jnp.sum(
            other * other, axis=-1, keepdims=True
        )
        inv_rms = lax.rsqrt(squares / (2 * half) + 1e-05)
        normed[:, own_columns] = (own * inv_rms).astype(jnp.bfloat16)
        normed[:, other_columns] = (other * inv_rms).astype(jnp.bfloat16)
        total[...] = jnp.zeros_like(total)

    rows = normed[...]
    gate = jnp.dot(rows, gate_ref[...], preferred_element_type=jnp.float32)
    up = jnp.dot(rows, up_ref[...], preferred_element_type=jnp.float32)
    units = (jax.nn.silu(gate) * up).astype(jnp.bfloat16)
    total[...] += jnp.dot(units, down_ref[...], preferred_element_type=jnp.float32)

    @pl.when(step == pl.num_programs(0) - 1)
    def _():
        kept_ref[...] = total[:, own_columns].reshape(kept_ref.shape)
        sent_ref[...] = total[:, other_columns].reshape(sent_ref.shape).astype(jnp.bfloat16)


def combine_kernel(
    experts, returned_ref, outgoing_ref, meta_ref, meta_other_ref, routes_ref, out_ref
):
    devices, rows, half = returned_ref.shape
    batches, per_batch, _ = out_ref.shape
    owners = devices // experts
    meta = meta_ref[...] + meta_other_ref[...]
    squares = meta[:, experts : experts + 1]
    inv_rms = lax.rsqrt(squares / (2 * half) + 1e-05)
    logits = meta * inv_rms
    chosen = jnp.concatenate([routes_ref[b] for b in range(batches)], axis=0)
    lane = lax.broadcasted_iota(jnp.int32, (rows, LANES), 1)
    first, second = chosen[:, 0:1], chosen[:, 1:2]
    logit_first = jnp.sum(jnp.where(lane == first, logits, 0.0), axis=-1, keepdims=True)
    logit_second = jnp.sum(jnp.where(lane == second, logits, 0.0), axis=-1, keepdims=True)
    gate_first = jax.nn.sigmoid(logit_first - logit_second)
    gate_second = jax.nn.sigmoid(logit_second - logit_first)
    result = outgoing_ref[0].astype(jnp.float32)
    for e in range(experts):
        expert_out = returned_ref[e * owners].astype(jnp.float32)
        for o in range(1, owners):
            expert_out += returned_ref[e * owners + o].astype(jnp.float32)
        weight = jnp.where(first == e, gate_first, 0.0) + jnp.where(second == e, gate_second, 0.0)
        result += weight * expert_out
    for b in range(batches):
        out_ref[b] = result[b * per_batch : (b + 1) * per_batch].astype(jnp.bfloat16)


VMEM = pl.BlockSpec(memory_space=pltpu.VMEM)
SMEM = pl.BlockSpec(memory_space=pltpu.SMEM)


def swap_cores(value):
    return lax.ppermute(value, "pair", [(0, 1), (1, 0)])


def on_device(
    query, key_cache, value_cache, lengths, residual, router, routes, w_gate, w_up, w_down
):
    devices = lax.axis_size("devs")
    experts = router.shape[1]
    batches, per_batch, half = query.shape
    rows = batches * per_batch
    outgoing, meta = pl.pallas_call(
        attend_kernel,
        in_specs=[VMEM, VMEM, VMEM, SMEM, VMEM, VMEM],
        out_specs=[VMEM, VMEM],
        out_shape=[
            jax.ShapeDtypeStruct((devices, rows, half), jnp.bfloat16),
            jax.ShapeDtypeStruct((rows, LANES), jnp.float32),
        ],
        compiler_params=pltpu.CompilerParams(vmem_limit_bytes=16 << 20),
    )(query, key_cache, value_cache, lengths, residual, router)
    meta_other = swap_cores(meta)
    arrived = lax.all_to_all(outgoing, "devs", split_axis=0, concat_axis=0, tiled=True)
    arrived_other = swap_cores(arrived)

    units = w_gate.shape[1]
    block = min(512, units)
    whole = pl.BlockSpec(arrived.shape, lambda i, side: (0, 0, 0))
    kept, sent = pl.pallas_call(
        expert_kernel,
        grid_spec=pltpu.PrefetchScalarGridSpec(
            num_scalar_prefetch=1,
            grid=(units // block,),
            in_specs=[
                whole,
                whole,
                pl.BlockSpec((2 * half, block), lambda i, side: (0, i)),
                pl.BlockSpec((2 * half, block), lambda i, side: (0, i)),
                pl.BlockSpec((block, 2 * half), lambda i, side: (i, 0)),
            ],
            out_specs=[whole, whole],
            scratch_shapes=[
                pltpu.VMEM((devices * rows, 2 * half), jnp.bfloat16),
                pltpu.VMEM((devices * rows, 2 * half), jnp.float32),
            ],
        ),
        out_shape=[
            jax.ShapeDtypeStruct(arrived.shape, jnp.float32),
            jax.ShapeDtypeStruct(arrived.shape, jnp.bfloat16),
        ],
        compiler_params=pltpu.CompilerParams(vmem_limit_bytes=50 << 20),
    )(
        lax.axis_index("pair").astype(jnp.int32).reshape(1),
        arrived,
        arrived_other,
        w_gate,
        w_up,
        w_down,
    )
    received = swap_cores(sent)
    summed = (kept + received.astype(jnp.float32)).astype(jnp.bfloat16)
    returned = lax.all_to_all(summed, "devs", split_axis=0, concat_axis=0, tiled=True)
    return pl.pallas_call(
        functools.partial(combine_kernel, experts),
        in_specs=[VMEM] * 5,
        out_specs=VMEM,
        out_shape=jax.ShapeDtypeStruct(query.shape, jnp.bfloat16),
        compiler_params=pltpu.CompilerParams(vmem_limit_bytes=16 << 20),
    )(returned, outgoing, meta, meta_other, routes)


def solution(mesh):
    in_specs = (
        P(None, ("groups", "devs"), "pair"),
        P(None, ("groups", "devs"), None, "pair"),
        P(None, ("groups", "devs"), None, "pair"),
        P(None, ("groups", "devs")),
        P(None, ("groups", "devs"), "pair"),
        P("pair", None),
        P(None, ("groups", "devs"), None),
        P(None, ("devs", "pair")),
        P(None, ("devs", "pair")),
        P(("devs", "pair"), None),
    )
    out_specs = P(None, ("groups", "devs"), "pair")
    return jax.shard_map(
        on_device, mesh=mesh, in_specs=in_specs, out_specs=out_specs, check_vma=False
    )
```

```python
import functools
import math

import jax
import jax.numpy as jnp
from jax import lax
from jax.experimental import pallas as pl
from jax.experimental.pallas import tpu as pltpu
from jax.sharding import PartitionSpec as P

HD = 128
AHEAD = 2
LANES = 128


def attend_kernel(
    query_hbm,
    key_hbm,
    value_hbm,
    lengths_hbm,
    residual_hbm,
    router_hbm,
    routes_hbm,
    hidden_ref,
    meta_ref,
    query_ref,
    key_ref,
    value_ref,
    lengths_ref,
    residual_ref,
    router_ref,
    routes_ref,
    arrival,
):
    batches, per_batch, width = query_ref.shape
    rows = batches * per_batch
    cache_len = key_ref.shape[2]
    kv_local = key_ref.shape[3] // HD
    group = width // key_ref.shape[3]
    early = [(query_hbm, query_ref), (lengths_hbm, lengths_ref), (key_hbm, key_ref)]
    late = [
        (value_hbm, value_ref),
        (residual_hbm, residual_ref),
        (router_hbm, router_ref),
        (routes_hbm, routes_ref),
    ]
    copies = [
        pltpu.make_async_copy(source, target, arrival.at[i])
        for i, (source, target) in enumerate(early + late)
    ]
    for copy in copies:
        copy.start()
    for copy in copies[: len(early)]:
        copy.wait()

    def stacked(ref):
        return jnp.concatenate([ref[b].astype(jnp.float32) for b in range(batches)], axis=0)

    queries = stacked(query_ref)
    tall = group * rows
    row_of = lax.rem(lax.broadcasted_iota(jnp.int32, (tall, 1), 0), rows)
    position = lax.broadcasted_iota(jnp.int32, (tall, cache_len), 1)
    limit = jnp.zeros((tall, 1), jnp.int32)
    for r in range(rows):
        limit = jnp.where(row_of == r, lengths_ref[r // per_batch, r % per_batch], limit)
    live = position < limit
    pieces = []
    for k in range(kv_local):
        heads = jnp.concatenate(
            [queries[:, (k * group + j) * HD : (k * group + j + 1) * HD] for j in range(group)],
            axis=0,
        ).astype(jnp.bfloat16)
        columns = slice(k * HD, (k + 1) * HD)
        scores = jnp.zeros((tall, cache_len), jnp.float32)
        for r in range(rows):
            keys = key_ref[r // per_batch, r % per_batch, :, columns]
            part = lax.dot_general(
                heads, keys, (((1,), (1,)), ((), ())), preferred_element_type=jnp.float32
            )
            scores = jnp.where(row_of == r, part, scores)
        scores = jnp.where(live, scores * (1.0 / math.sqrt(HD)), -jnp.inf)
        peak = jnp.max(scores, axis=-1, keepdims=True)
        weights = jnp.where(live, jnp.exp(scores - peak), 0.0)
        total = jnp.sum(weights, axis=-1, keepdims=True)
        weights_bf = weights.astype(jnp.bfloat16)
        if k == 0:
            for copy in copies[len(early) :]:
                copy.wait()
        mixed = jnp.zeros((tall, HD), jnp.float32)
        for r in range(rows):
            values = value_ref[r // per_batch, r % per_batch, :, columns]
            part = jnp.dot(weights_bf, values, preferred_element_type=jnp.float32)
            mixed = jnp.where(row_of == r, part, mixed)
        mixed = mixed / total
        pieces += [mixed[j * rows : (j + 1) * rows] for j in range(group)]
    attended = jnp.concatenate(pieces, axis=1)
    hidden = (stacked(residual_ref) + attended).astype(jnp.bfloat16)
    wide = hidden.astype(jnp.float32)
    logits = lax.dot_general(
        hidden, router_ref[...], (((1,), (1,)), ((), ())), preferred_element_type=jnp.float32
    )
    squares = jnp.sum(wide * wide, axis=-1, keepdims=True)
    experts = router_ref.shape[0]
    row = lax.broadcasted_iota(jnp.int32, (rows, 1), 0)
    meta_ref[...] = jnp.zeros_like(meta_ref)
    meta_ref[:, :experts] = logits
    meta_ref[:, experts : experts + 1] = squares
    for which in range(2):
        route = jnp.zeros((rows, 1), jnp.int32)
        for r in range(rows):
            route = jnp.where(row == r, routes_ref[r // per_batch, which, r % per_batch], route)
        lane = experts + 1 + which
        meta_ref[:, lane : lane + 1] = route.astype(jnp.float32)
    hidden_ref[...] = hidden


def fetch_kernel(after_ref, meta_ref, source_hbm, target_ref, meta_out_ref, arrival):
    copy = pltpu.make_async_copy(
        source_hbm.at[:, pl.ds(0, target_ref.shape[1])], target_ref, arrival
    )
    copy.start()
    meta_out_ref[...] = meta_ref[...]
    copy.wait()


def stack_kernel(*refs):
    for i, ref in enumerate(refs[:-2]):
        refs[-1][i] = ref[...]


def expert_kernel(
    offsets,
    *refs,
):
    parts = (len(refs) - 13) // 2
    own_refs, other_refs = refs[:parts], refs[parts : 2 * parts]
    (
        gate_ref,
        first_up_ref,
        up_hbm,
        down_hbm,
        kept_ref,
        sent_ref,
        normed,
        gates,
        units_bf,
        up_ref,
        down_ref,
        up_arrival,
        down_arrival,
    ) = refs[2 * parts :]
    count, width = normed.shape
    half = width // 2
    units = gate_ref.shape[1]
    block = min(512, units)
    first = first_up_ref.shape[1]
    me = lax.axis_index("devs")
    side = lax.axis_index("pair")
    own_start = pl.multiple_of(side * half, LANES)
    other_start = pl.multiple_of((1 - side) * half, LANES)

    up_copies = []
    for i, start in enumerate(range(first, units, block)):
        up_copies.append(
            pltpu.make_async_copy(
                up_hbm.at[:, pl.ds(start, block)], up_ref.at[i], up_arrival.at[i]
            )
        )
    down_copies = []
    slices = down_ref.shape[0]
    piece = down_ref.shape[2]
    for i in range(slices):
        base = other_start if i < slices // 2 else own_start
        start = pl.multiple_of(base + (i % (slices // 2)) * piece, LANES)
        down_copies.append(
            pltpu.make_async_copy(
                down_hbm.at[:, pl.ds(start, piece)], down_ref.at[i], down_arrival.at[i]
            )
        )
    copies = up_copies + down_copies
    for copy in copies[:AHEAD]:
        copy.start()

    def wait(i):
        copies[i].wait()
        if i + AHEAD < len(copies):
            copies[i + AHEAD].start()

    def rows_of(refs):
        tall = [ref[...].astype(jnp.float32).reshape(-1, half) for ref in refs]
        return jnp.concatenate(tall, axis=0)

    own, other = rows_of(own_refs), rows_of(other_refs)
    squares = jnp.sum(own * own, axis=-1, keepdims=True) + jnp.sum(
        other * other, axis=-1, keepdims=True
    )
    inv_rms = lax.rsqrt(squares / width + 1e-05)
    normed[:, pl.ds(own_start, half)] = (own * inv_rms).astype(jnp.bfloat16)
    normed[:, pl.ds(other_start, half)] = (other * inv_rms).astype(jnp.bfloat16)

    for start in range(0, units, block):
        part = slice(start, start + block)
        gate = jnp.dot(normed[...], gate_ref[:, part], preferred_element_type=jnp.float32)
        gates[:, part] = jax.nn.silu(gate)
    for start in range(0, units, block):
        part = slice(start, start + block)
        if start < first:
            held = first_up_ref[:, part]
        else:
            i = (start - first) // block
            wait(i)
            held = up_ref[i]
        up = jnp.dot(normed[...], held, preferred_element_type=jnp.float32)
        units_bf[:, part] = (gates[:, part] * up).astype(jnp.bfloat16)
    rows = count // len(offsets)
    for i in range(slices):
        wait(len(up_copies) + i)
        product = jnp.dot(units_bf[...], down_ref[i], preferred_element_type=jnp.float32)
        columns = slice(i % (slices // 2) * piece, (i % (slices // 2) + 1) * piece)
        target = sent_ref if i < slices // 2 else kept_ref
        for j, offset in enumerate(offsets):
            target[lax.bitwise_xor(me, offset), :, columns] = product[
                j * rows : (j + 1) * rows
            ].astype(target.dtype)


def combine_kernel(
    experts, returned_ref, hidden_ref, meta_ref, meta_other_ref, out_ref
):
    devices, rows, half = returned_ref.shape
    batches, per_batch, _ = out_ref.shape
    owners = devices // experts
    meta = meta_ref[...] + meta_other_ref[...]
    squares = meta[:, experts : experts + 1]
    inv_rms = lax.rsqrt(squares / (2 * half) + 1e-05)
    logits = meta * inv_rms
    chosen = meta_ref[:, experts + 1 : experts + 3].astype(jnp.int32)
    lane = lax.broadcasted_iota(jnp.int32, (rows, LANES), 1)
    first, second = chosen[:, 0:1], chosen[:, 1:2]
    logit_first = jnp.sum(jnp.where(lane == first, logits, 0.0), axis=-1, keepdims=True)
    logit_second = jnp.sum(jnp.where(lane == second, logits, 0.0), axis=-1, keepdims=True)
    gate_first = jax.nn.sigmoid(logit_first - logit_second)
    gate_second = jax.nn.sigmoid(logit_second - logit_first)
    result = hidden_ref[...].astype(jnp.float32)
    for e in range(experts):
        expert_out = returned_ref[e * owners].astype(jnp.float32)
        for o in range(1, owners):
            expert_out += returned_ref[e * owners + o].astype(jnp.float32)
        weight = jnp.where(first == e, gate_first, 0.0) + jnp.where(second == e, gate_second, 0.0)
        result += weight * expert_out
    for b in range(batches):
        out_ref[b] = result[b * per_batch : (b + 1) * per_batch].astype(jnp.bfloat16)


VMEM = pl.BlockSpec(memory_space=pltpu.VMEM)
HBM = pl.BlockSpec(memory_space=pltpu.HBM)


def far(array):
    return pltpu.with_memory_space_constraint(array, pltpu.HBM)


def fetch(meta, weights, columns, after=None):
    after = meta if after is None else after
    near = jax.ShapeDtypeStruct((weights.shape[0], columns), weights.dtype)
    return pl.pallas_call(
        fetch_kernel,
        in_specs=[VMEM, VMEM, HBM],
        out_specs=[VMEM, VMEM],
        out_shape=[near, jax.ShapeDtypeStruct(meta.shape, meta.dtype)],
        scratch_shapes=[pltpu.SemaphoreType.DMA],
        compiler_params=pltpu.CompilerParams(vmem_limit_bytes=1 << 20),
        cost_estimate=pl.CostEstimate(
            flops=0, bytes_accessed=2 * near.size, transcendentals=0
        ),
    )(after, meta, far(weights))


def swap_devices(value, offset, devices):
    return lax.ppermute(value, "devs", [(d, d ^ offset) for d in range(devices)])


def swap_cores(value):
    return lax.ppermute(value, "pair", [(0, 1), (1, 0)])


def on_device(
    query, key_cache, value_cache, lengths, residual, router, routes, w_gate, w_up, w_down
):
    devices = lax.axis_size("devs")
    experts = router.shape[1]
    batches, per_batch, half = query.shape
    rows = batches * per_batch
    inputs = (
        query,
        key_cache,
        value_cache,
        lengths,
        residual,
        jnp.transpose(router),
        jnp.transpose(routes, (0, 2, 1)),
    )
    hidden, meta = pl.pallas_call(
        attend_kernel,
        in_specs=[HBM] * 7,
        out_specs=[VMEM, VMEM],
        out_shape=[
            jax.ShapeDtypeStruct((rows, half), jnp.bfloat16),
            jax.ShapeDtypeStruct((rows, LANES), jnp.float32),
        ],
        scratch_shapes=[
            (pltpu.SMEM if array.dtype == jnp.int32 else pltpu.VMEM)(array.shape, array.dtype)
            for array in inputs
        ]
        + [pltpu.SemaphoreType.DMA((7,))],
        compiler_params=pltpu.CompilerParams(vmem_limit_bytes=16 << 20),
    )(*[far(array) for array in inputs])
    width, units = w_gate.shape
    block = min(512, units)
    first = min(1024, units)
    piece = min(512, half)
    count = devices * rows
    owners = devices // experts

    offsets = [k * owners for k in range(experts)]
    crossed = [swap_devices(hidden, offset, devices) for offset in offsets[1:]]
    gate_near, meta = fetch(meta, w_gate, units)
    held = [
        pl.pallas_call(
            stack_kernel,
            in_specs=[VMEM] * (experts + 1),
            out_specs=VMEM,
            out_shape=jax.ShapeDtypeStruct((experts, rows, half), jnp.bfloat16),
            compiler_params=pltpu.CompilerParams(vmem_limit_bytes=2 << 20),
        )(hidden, *crossed, meta)
    ]
    step = 1
    while step < owners:
        if len(held) > 1:
            held = [jnp.concatenate(held, axis=0)]
        held.append(swap_devices(held[0], step, devices))
        offsets += [offset ^ step for offset in offsets]
        step *= 2
    up_near, meta = fetch(meta, w_up, first, held[0])
    others = [swap_cores(held[0])]
    if len(held) > 1:
        held[1], meta = lax.optimization_barrier((held[1], meta))
        others.append(swap_cores(held[1]))
    meta_other = swap_cores(meta)
    kept, sent = pl.pallas_call(
        functools.partial(expert_kernel, offsets),
        in_specs=[VMEM] * (2 * len(held) + 2) + [HBM] * 2,
        out_specs=[VMEM, VMEM],
        out_shape=[
            jax.ShapeDtypeStruct((devices, rows, half), jnp.float32),
            jax.ShapeDtypeStruct((devices, rows, half), jnp.bfloat16),
        ],
        scratch_shapes=[
            pltpu.VMEM((count, width), jnp.bfloat16),
            pltpu.VMEM((count, units), jnp.float32),
            pltpu.VMEM((count, units), jnp.bfloat16),
            pltpu.VMEM((max(1, (units - first) // block), width, block), jnp.bfloat16),
            pltpu.VMEM((width // piece, units, piece), jnp.bfloat16),
            pltpu.SemaphoreType.DMA((max(1, (units - first) // block),)),
            pltpu.SemaphoreType.DMA((width // piece,)),
        ],
        compiler_params=pltpu.CompilerParams(vmem_limit_bytes=32 << 20),
    )(*held, *others, gate_near, up_near, far(w_up), far(w_down))
    received = swap_cores(sent)
    summed = (kept + received.astype(jnp.float32)).astype(jnp.bfloat16)
    returned = lax.all_to_all(summed, "devs", split_axis=0, concat_axis=0, tiled=True)
    return pl.pallas_call(
        functools.partial(combine_kernel, experts),
        in_specs=[VMEM] * 4,
        out_specs=VMEM,
        out_shape=jax.ShapeDtypeStruct(query.shape, jnp.bfloat16),
        compiler_params=pltpu.CompilerParams(vmem_limit_bytes=16 << 20),
    )(returned, hidden, meta, meta_other)


def solution(mesh):
    in_specs = (
        P(None, ("groups", "devs"), "pair"),
        P(None, ("groups", "devs"), None, "pair"),
        P(None, ("groups", "devs"), None, "pair"),
        P(None, ("groups", "devs")),
        P(None, ("groups", "devs"), "pair"),
        P("pair", None),
        P(None, ("groups", "devs"), None),
        P(None, ("devs", "pair")),
        P(None, ("devs", "pair")),
        P(("devs", "pair"), None),
    )
    out_specs = P(None, ("groups", "devs"), "pair")
    return jax.shard_map(
        on_device, mesh=mesh, in_specs=in_specs, out_specs=out_specs, check_vma=False
    )
```

```python
import functools
import math

import jax
import jax.numpy as jnp
from jax import lax
from jax.experimental import pallas as pl
from jax.experimental.pallas import tpu as pltpu
from jax.sharding import PartitionSpec as P

HD = 128
LANES = 128


def attend_kernel(
    query_hbm,
    key_hbm,
    value_hbm,
    lengths_hbm,
    residual_hbm,
    router_hbm,
    routes_hbm,
    hidden_ref,
    meta_ref,
    query_ref,
    key_ref,
    value_ref,
    lengths_ref,
    residual_ref,
    router_ref,
    routes_ref,
    arrival,
):
    batches, per_batch, width = query_ref.shape
    rows = batches * per_batch
    cache_len = key_ref.shape[2]
    kv_local = key_ref.shape[3] // HD
    group = width // key_ref.shape[3]
    early = [(query_hbm, query_ref), (lengths_hbm, lengths_ref), (key_hbm, key_ref)]
    late = [
        (value_hbm, value_ref),
        (residual_hbm, residual_ref),
        (router_hbm, router_ref),
        (routes_hbm, routes_ref),
    ]
    copies = [
        pltpu.make_async_copy(source, target, arrival.at[i])
        for i, (source, target) in enumerate(early + late)
    ]
    for copy in copies:
        copy.start()
    for copy in copies[: len(early)]:
        copy.wait()

    def stacked(ref):
        return jnp.concatenate([ref[b].astype(jnp.float32) for b in range(batches)], axis=0)

    queries = stacked(query_ref)
    tall = group * rows
    row_of = lax.rem(lax.broadcasted_iota(jnp.int32, (tall, 1), 0), rows)
    position = lax.broadcasted_iota(jnp.int32, (tall, cache_len), 1)
    limit = jnp.zeros((tall, 1), jnp.int32)
    for r in range(rows):
        limit = jnp.where(row_of == r, lengths_ref[r // per_batch, r % per_batch], limit)
    live = position < limit
    pieces = []
    for k in range(kv_local):
        heads = jnp.concatenate(
            [queries[:, (k * group + j) * HD : (k * group + j + 1) * HD] for j in range(group)],
            axis=0,
        ).astype(jnp.bfloat16)
        columns = slice(k * HD, (k + 1) * HD)
        scores = jnp.zeros((tall, cache_len), jnp.float32)
        for r in range(rows):
            keys = key_ref[r // per_batch, r % per_batch, :, columns]
            part = lax.dot_general(
                heads, keys, (((1,), (1,)), ((), ())), preferred_element_type=jnp.float32
            )
            scores = jnp.where(row_of == r, part, scores)
        scores = jnp.where(live, scores * (1.0 / math.sqrt(HD)), -jnp.inf)
        peak = jnp.max(scores, axis=-1, keepdims=True)
        weights = jnp.where(live, jnp.exp(scores - peak), 0.0)
        total = jnp.sum(weights, axis=-1, keepdims=True)
        weights_bf = weights.astype(jnp.bfloat16)
        if k == 0:
            for copy in copies[len(early) :]:
                copy.wait()
        mixed = jnp.zeros((tall, HD), jnp.float32)
        for r in range(rows):
            values = value_ref[r // per_batch, r % per_batch, :, columns]
            part = jnp.dot(weights_bf, values, preferred_element_type=jnp.float32)
            mixed = jnp.where(row_of == r, part, mixed)
        mixed = mixed / total
        pieces += [mixed[j * rows : (j + 1) * rows] for j in range(group)]
    attended = jnp.concatenate(pieces, axis=1)
    hidden = (stacked(residual_ref) + attended).astype(jnp.bfloat16)
    wide = hidden.astype(jnp.float32)
    logits = lax.dot_general(
        hidden, router_ref[...], (((1,), (1,)), ((), ())), preferred_element_type=jnp.float32
    )
    squares = jnp.sum(wide * wide, axis=-1, keepdims=True)
    experts = router_ref.shape[0]
    row = lax.broadcasted_iota(jnp.int32, (rows, 1), 0)
    meta_ref[...] = jnp.zeros_like(meta_ref)
    meta_ref[:, :experts] = logits
    meta_ref[:, experts : experts + 1] = squares
    for which in range(2):
        route = jnp.zeros((rows, 1), jnp.int32)
        for r in range(rows):
            route = jnp.where(row == r, routes_ref[r // per_batch, which, r % per_batch], route)
        lane = experts + 1 + which
        meta_ref[:, lane : lane + 1] = route.astype(jnp.float32)
    hidden_ref[...] = hidden


def fetch_kernel(starts, after_ref, meta_ref, *refs):
    count = len(starts)
    sources, targets, meta_out_ref, arrival = (
        refs[:count],
        refs[count : 2 * count],
        refs[2 * count],
        refs[2 * count + 1],
    )
    copies = [
        pltpu.make_async_copy(
            source.at[pl.ds(start, target.shape[0])], target, arrival.at[i]
        )
        for i, (start, source, target) in enumerate(zip(starts, sources, targets))
    ]
    for copy in copies:
        copy.start()
    meta_out_ref[...] = meta_ref[...]
    for copy in copies:
        copy.wait()


def stack_kernel(*refs):
    for i, ref in enumerate(refs[:-2]):
        refs[-1][i] = ref[...]


def rows_of(refs):
    half = refs[0].shape[-1]
    tall = [ref[...].astype(jnp.float32).reshape(-1, half) for ref in refs]
    return jnp.concatenate(tall, axis=0)


def half_starts(half):
    side = lax.axis_index("pair")
    return (
        pl.multiple_of(side * half, LANES),
        pl.multiple_of((1 - side) * half, LANES),
    )


def gate_kernel(block, *refs):
    *own_refs, gate_ref, down_hbm, gates_ref, down_ref, arrival = refs
    half = own_refs[0].shape[-1]
    units = gate_ref.shape[1]
    own_start, _ = half_starts(half)
    copy = pltpu.make_async_copy(down_hbm.at[pl.ds(0, block)], down_ref, arrival)
    copy.start()
    rows = rows_of(own_refs).astype(jnp.bfloat16)
    for start in range(0, units, block):
        part = slice(start, start + block)
        gates_ref[:, part] = jnp.dot(
            rows, gate_ref[pl.ds(own_start, half), part], preferred_element_type=jnp.float32
        )
    copy.wait()


def store_rows(offsets, target, columns, product):
    me = lax.axis_index("devs")
    rows = target.shape[1]
    for j, offset in enumerate(offsets):
        target[lax.bitwise_xor(me, offset), :, columns] = product[
            j * rows : (j + 1) * rows
        ].astype(target.dtype)


def down_dot(units_ref, down_refs, columns):
    total, start = None, 0
    for ref in down_refs:
        stop = start + ref.shape[0]
        product = jnp.dot(
            units_ref[:, start:stop], ref[:, columns], preferred_element_type=jnp.float32
        )
        total = product if total is None else total + product
        start = stop
    return total


def expert_kernel(block, piece, offsets, parts, *refs):
    own_refs, refs = refs[:parts], refs[parts:]
    other_refs, refs = refs[:parts], refs[parts:]
    (
        up_early_ref,
        up_late_ref,
        gate_ref,
        gates_ref,
        down_early_ref,
        meta_other_ref,
        down_hbm,
        sent_ref,
        units_ref,
        down_late_ref,
        rows_ref,
        arrival,
    ) = refs
    width = rows_ref.shape[1]
    half = width // 2
    units = gate_ref.shape[1]
    early = up_early_ref.shape[0]
    own_start, other_start = half_starts(half)
    pending = []
    for i, start in enumerate(range(block, units, block)):
        pending.append(
            pltpu.make_async_copy(
                down_hbm.at[pl.ds(start, block)],
                down_late_ref.at[pl.ds(start - block, block)],
                arrival.at[i],
            )
        )
    copies = list(pending)
    for copy in copies:
        copy.start()

    own, other = rows_of(own_refs), rows_of(other_refs)
    squares = jnp.sum(own * own, axis=-1, keepdims=True) + jnp.sum(
        other * other, axis=-1, keepdims=True
    )
    inv_rms = lax.rsqrt(squares / width + 1e-05)
    other = other.astype(jnp.bfloat16)
    rows_ref[:, pl.ds(own_start, half)] = own.astype(jnp.bfloat16)
    rows_ref[:, pl.ds(other_start, half)] = other

    for start in range(0, units, block):
        part = slice(start, start + block)
        gate = gates_ref[:, part] + jnp.dot(
            other, gate_ref[pl.ds(other_start, half), part], preferred_element_type=jnp.float32
        )
        gate = jax.nn.silu(gate * inv_rms) * inv_rms
        up = jnp.dot(
            rows_ref[:, :early], up_early_ref[:, part], preferred_element_type=jnp.float32
        ) + jnp.dot(
            rows_ref[:, early:], up_late_ref[:, part], preferred_element_type=jnp.float32
        )
        units_ref[:, part] = (gate * up).astype(jnp.bfloat16)
    for copy in copies:
        copy.wait()
    downs = [down_early_ref] + [down_late_ref] * (units > block)
    for start in range(0, half, piece):
        columns = pl.ds(pl.multiple_of(other_start + start, LANES), piece)
        product = down_dot(units_ref, downs, columns)
        store_rows(offsets, sent_ref, slice(start, start + piece), product)


def keep_kernel(block, piece, offsets, units_ref, down_early_ref, down_late_ref, kept_ref):
    half = kept_ref.shape[-1]
    own_start, _ = half_starts(half)
    downs = [down_early_ref] + [down_late_ref] * (units_ref.shape[1] > block)
    for start in range(0, half, piece):
        columns = pl.ds(pl.multiple_of(own_start + start, LANES), piece)
        product = down_dot(units_ref, downs, columns)
        store_rows(offsets, kept_ref, slice(start, start + piece), product)


def add_kernel(kept_ref, received_ref, out_ref):
    out_ref[...] = (kept_ref[...] + received_ref[...].astype(jnp.float32)).astype(jnp.bfloat16)


def combine_kernel(
    experts, returned_ref, hidden_ref, meta_ref, meta_other_ref, out_ref
):
    devices, rows, half = returned_ref.shape
    batches, per_batch, _ = out_ref.shape
    owners = devices // experts
    meta = meta_ref[...] + meta_other_ref[...]
    squares = meta[:, experts : experts + 1]
    inv_rms = lax.rsqrt(squares / (2 * half) + 1e-05)
    logits = meta * inv_rms
    chosen = meta_ref[:, experts + 1 : experts + 3].astype(jnp.int32)
    lane = lax.broadcasted_iota(jnp.int32, (rows, LANES), 1)
    first, second = chosen[:, 0:1], chosen[:, 1:2]
    logit_first = jnp.sum(jnp.where(lane == first, logits, 0.0), axis=-1, keepdims=True)
    logit_second = jnp.sum(jnp.where(lane == second, logits, 0.0), axis=-1, keepdims=True)
    gate_first = jax.nn.sigmoid(logit_first - logit_second)
    gate_second = jax.nn.sigmoid(logit_second - logit_first)
    result = hidden_ref[...].astype(jnp.float32)
    for e in range(experts):
        expert_out = returned_ref[e * owners].astype(jnp.float32)
        for o in range(1, owners):
            expert_out += returned_ref[e * owners + o].astype(jnp.float32)
        weight = jnp.where(first == e, gate_first, 0.0) + jnp.where(second == e, gate_second, 0.0)
        result += weight * expert_out
    for b in range(batches):
        out_ref[b] = result[b * per_batch : (b + 1) * per_batch].astype(jnp.bfloat16)


VMEM = pl.BlockSpec(memory_space=pltpu.VMEM)
HBM = pl.BlockSpec(memory_space=pltpu.HBM)


def far(array):
    return pltpu.with_memory_space_constraint(array, pltpu.HBM)


def fetch(meta, after, *wanted):
    near = [
        jax.ShapeDtypeStruct((count, weights.shape[1]), weights.dtype)
        for weights, _, count in wanted
    ]
    *loaded, meta = pl.pallas_call(
        functools.partial(fetch_kernel, [start for _, start, _ in wanted]),
        in_specs=[VMEM, VMEM] + [HBM] * len(wanted),
        out_specs=[VMEM] * (len(wanted) + 1),
        out_shape=near + [jax.ShapeDtypeStruct(meta.shape, meta.dtype)],
        scratch_shapes=[pltpu.SemaphoreType.DMA((len(wanted),))],
        compiler_params=pltpu.CompilerParams(vmem_limit_bytes=1 << 20),
        cost_estimate=pl.CostEstimate(
            flops=0, bytes_accessed=2 * sum(array.size for array in near), transcendentals=0
        ),
    )(after, meta, *[far(weights) for weights, _, _ in wanted])
    return loaded, meta


def swap_devices(value, offset, devices):
    return lax.ppermute(value, "devs", [(d, d ^ offset) for d in range(devices)])


def swap_cores(value):
    return lax.ppermute(value, "pair", [(0, 1), (1, 0)])


def on_device(
    query, key_cache, value_cache, lengths, residual, router, routes, w_gate, w_up, w_down
):
    devices = lax.axis_size("devs")
    experts = router.shape[1]
    batches, per_batch, half = query.shape
    rows = batches * per_batch
    inputs = (
        query,
        key_cache,
        value_cache,
        lengths,
        residual,
        jnp.transpose(router),
        jnp.transpose(routes, (0, 2, 1)),
    )
    width, units = w_gate.shape
    block = min(512, units)
    early = width // 4
    piece = min(512, half)
    count = devices * rows
    owners = devices // experts
    hidden, meta = pl.pallas_call(
        attend_kernel,
        in_specs=[HBM] * 7,
        out_specs=[VMEM] * 2,
        out_shape=[
            jax.ShapeDtypeStruct((rows, half), jnp.bfloat16),
            jax.ShapeDtypeStruct((rows, LANES), jnp.float32),
        ],
        scratch_shapes=[
            (pltpu.SMEM if array.dtype == jnp.int32 else pltpu.VMEM)(array.shape, array.dtype)
            for array in inputs
        ]
        + [pltpu.SemaphoreType.DMA((7,))],
        compiler_params=pltpu.CompilerParams(vmem_limit_bytes=16 << 20),
    )(*[far(array) for array in inputs])

    offsets = [k * owners for k in range(experts)]
    crossed = [swap_devices(hidden, offset, devices) for offset in offsets[1:]]
    gate_near = pltpu.with_memory_space_constraint(w_gate, pltpu.VMEM)
    (up_early,), meta = fetch(meta, meta, (w_up, 0, early))
    held = [
        pl.pallas_call(
            stack_kernel,
            in_specs=[VMEM] * (experts + 1),
            out_specs=VMEM,
            out_shape=jax.ShapeDtypeStruct((experts, rows, half), jnp.bfloat16),
            compiler_params=pltpu.CompilerParams(vmem_limit_bytes=2 << 20),
        )(hidden, *crossed, meta)
    ]
    step = 1
    while step < owners:
        if len(held) > 1:
            held = [jnp.concatenate(held, axis=0)]
        held.append(swap_devices(held[0], step, devices))
        offsets += [offset ^ step for offset in offsets]
        step *= 2
    (up_late,), meta = fetch(meta, held[0], (w_up, early, width - early))
    others = [swap_cores(held[0])]
    if len(held) > 1:
        held[1], meta = lax.optimization_barrier((held[1], meta))
        others.append(swap_cores(held[1]))
    meta_other = swap_cores(meta)
    parts = len(held)
    gates, down_early = pl.pallas_call(
        functools.partial(gate_kernel, block),
        in_specs=[VMEM] * (parts + 1) + [HBM],
        out_specs=[VMEM, VMEM],
        out_shape=[
            jax.ShapeDtypeStruct((count, units), jnp.float32),
            jax.ShapeDtypeStruct((block, width), jnp.bfloat16),
        ],
        scratch_shapes=[pltpu.SemaphoreType.DMA],
        compiler_params=pltpu.CompilerParams(vmem_limit_bytes=min(48, count // 16) << 20),
        cost_estimate=pl.CostEstimate(
            flops=2 * count * half * units, bytes_accessed=2 * half * units, transcendentals=0
        ),
    )(*held, gate_near, far(w_down))
    late = max(block, units - block)
    sent, units_bf, down_late = pl.pallas_call(
        functools.partial(expert_kernel, block, piece, offsets, parts),
        in_specs=[VMEM] * (2 * parts + 6) + [HBM],
        out_specs=[VMEM] * 3,
        out_shape=[
            jax.ShapeDtypeStruct((devices, rows, half), jnp.bfloat16),
            jax.ShapeDtypeStruct((count, units), jnp.bfloat16),
            jax.ShapeDtypeStruct((late, width), jnp.bfloat16),
        ],
        scratch_shapes=[
            pltpu.VMEM((count, width), jnp.bfloat16),
            pltpu.SemaphoreType.DMA((late // block,)),
        ],
        compiler_params=pltpu.CompilerParams(vmem_limit_bytes=min(48, count // 8) << 20),
    )(*held, *others, up_early, up_late, gate_near, gates, down_early, meta_other, far(w_down))
    received = swap_cores(sent)
    kept = pl.pallas_call(
        functools.partial(keep_kernel, block, piece, offsets),
        in_specs=[VMEM] * 3,
        out_specs=VMEM,
        out_shape=jax.ShapeDtypeStruct((devices, rows, half), jnp.float32),
        compiler_params=pltpu.CompilerParams(vmem_limit_bytes=min(48, count // 16) << 20),
        cost_estimate=pl.CostEstimate(
            flops=2 * count * half * units, bytes_accessed=2 * half * units, transcendentals=0
        ),
    )(units_bf, down_early, down_late)
    summed = pl.pallas_call(
        add_kernel,
        in_specs=[VMEM] * 2,
        out_specs=VMEM,
        out_shape=jax.ShapeDtypeStruct((devices, rows, half), jnp.bfloat16),
        compiler_params=pltpu.CompilerParams(vmem_limit_bytes=min(48, count // 16) << 20),
    )(kept, received)
    returned = lax.all_to_all(summed, "devs", split_axis=0, concat_axis=0, tiled=True)
    return pl.pallas_call(
        functools.partial(combine_kernel, experts),
        in_specs=[VMEM] * 4,
        out_specs=VMEM,
        out_shape=jax.ShapeDtypeStruct(query.shape, jnp.bfloat16),
        compiler_params=pltpu.CompilerParams(vmem_limit_bytes=16 << 20),
    )(returned, hidden, meta, meta_other)


def solution(mesh):
    in_specs = (
        P(None, ("groups", "devs"), "pair"),
        P(None, ("groups", "devs"), None, "pair"),
        P(None, ("groups", "devs"), None, "pair"),
        P(None, ("groups", "devs")),
        P(None, ("groups", "devs"), "pair"),
        P("pair", None),
        P(None, ("groups", "devs"), None),
        P(None, ("devs", "pair")),
        P(None, ("devs", "pair")),
        P(("devs", "pair"), None),
    )
    out_specs = P(None, ("groups", "devs"), "pair")
    return jax.shard_map(
        on_device, mesh=mesh, in_specs=in_specs, out_specs=out_specs, check_vma=False
    )
```

```python
import functools
import math

import jax
import jax.numpy as jnp
from jax import lax
from jax.experimental import pallas as pl
from jax.experimental.pallas import tpu as pltpu
from jax.sharding import PartitionSpec as P

HD = 128
LANES = 128


def attend_kernel(
    query_hbm,
    key_hbm,
    value_hbm,
    lengths_hbm,
    residual_hbm,
    router_hbm,
    routes_hbm,
    hidden_ref,
    meta_ref,
    query_ref,
    key_ref,
    value_ref,
    lengths_ref,
    residual_ref,
    router_ref,
    routes_ref,
    arrival,
):
    batches, per_batch, width = query_ref.shape
    rows = batches * per_batch
    cache_len = key_ref.shape[2]
    kv_local = key_ref.shape[3] // HD
    group = width // key_ref.shape[3]
    early = [(query_hbm, query_ref), (lengths_hbm, lengths_ref), (key_hbm, key_ref)]
    late = [
        (value_hbm, value_ref),
        (residual_hbm, residual_ref),
        (router_hbm, router_ref),
        (routes_hbm, routes_ref),
    ]
    copies = [
        pltpu.make_async_copy(source, target, arrival.at[i])
        for i, (source, target) in enumerate(early + late)
    ]
    for copy in copies:
        copy.start()
    for copy in copies[: len(early)]:
        copy.wait()

    def stacked(ref):
        return jnp.concatenate([ref[b].astype(jnp.float32) for b in range(batches)], axis=0)

    queries = stacked(query_ref)
    tall = group * rows
    row_of = lax.rem(lax.broadcasted_iota(jnp.int32, (tall, 1), 0), rows)
    position = lax.broadcasted_iota(jnp.int32, (tall, cache_len), 1)
    limit = jnp.zeros((tall, 1), jnp.int32)
    for r in range(rows):
        limit = jnp.where(row_of == r, lengths_ref[r // per_batch, r % per_batch], limit)
    live = position < limit
    pieces = []
    for k in range(kv_local):
        heads = jnp.concatenate(
            [queries[:, (k * group + j) * HD : (k * group + j + 1) * HD] for j in range(group)],
            axis=0,
        ).astype(jnp.bfloat16)
        columns = slice(k * HD, (k + 1) * HD)
        scores = jnp.zeros((tall, cache_len), jnp.float32)
        for r in range(rows):
            keys = key_ref[r // per_batch, r % per_batch, :, columns]
            part = lax.dot_general(
                heads, keys, (((1,), (1,)), ((), ())), preferred_element_type=jnp.float32
            )
            scores = jnp.where(row_of == r, part, scores)
        scores = jnp.where(live, scores * (1.0 / math.sqrt(HD)), -jnp.inf)
        peak = jnp.max(scores, axis=-1, keepdims=True)
        weights = jnp.where(live, jnp.exp(scores - peak), 0.0)
        total = jnp.sum(weights, axis=-1, keepdims=True)
        weights_bf = weights.astype(jnp.bfloat16)
        if k == 0:
            for copy in copies[len(early) :]:
                copy.wait()
        mixed = jnp.zeros((tall, HD), jnp.float32)
        for r in range(rows):
            values = value_ref[r // per_batch, r % per_batch, :, columns]
            part = jnp.dot(weights_bf, values, preferred_element_type=jnp.float32)
            mixed = jnp.where(row_of == r, part, mixed)
        mixed = mixed / total
        pieces += [mixed[j * rows : (j + 1) * rows] for j in range(group)]
    attended = jnp.concatenate(pieces, axis=1)
    hidden = (stacked(residual_ref) + attended).astype(jnp.bfloat16)
    wide = hidden.astype(jnp.float32)
    logits = lax.dot_general(
        hidden, router_ref[...], (((1,), (1,)), ((), ())), preferred_element_type=jnp.float32
    )
    squares = jnp.sum(wide * wide, axis=-1, keepdims=True)
    experts = router_ref.shape[0]
    row = lax.broadcasted_iota(jnp.int32, (rows, 1), 0)
    meta_ref[...] = jnp.zeros_like(meta_ref)
    meta_ref[:, :experts] = logits
    meta_ref[:, experts : experts + 1] = squares
    for which in range(2):
        route = jnp.zeros((rows, 1), jnp.int32)
        for r in range(rows):
            route = jnp.where(row == r, routes_ref[r // per_batch, which, r % per_batch], route)
        lane = experts + 1 + which
        meta_ref[:, lane : lane + 1] = route.astype(jnp.float32)
    hidden_ref[...] = hidden


def fetch_kernel(starts, after_ref, meta_ref, *refs):
    count = len(starts)
    sources, targets, meta_out_ref, arrival = (
        refs[:count],
        refs[count : 2 * count],
        refs[2 * count],
        refs[2 * count + 1],
    )
    copies = [
        pltpu.make_async_copy(
            source.at[pl.ds(start, target.shape[0])], target, arrival.at[i]
        )
        for i, (start, source, target) in enumerate(zip(starts, sources, targets))
    ]
    for copy in copies:
        copy.start()
    meta_out_ref[...] = meta_ref[...]
    for copy in copies:
        copy.wait()


def stack_kernel(*refs):
    for i, ref in enumerate(refs[:-2]):
        refs[-1][i] = ref[...]


def rows_of(refs):
    half = refs[0].shape[-1]
    tall = [ref[...].astype(jnp.float32).reshape(-1, half) for ref in refs]
    return jnp.concatenate(tall, axis=0)


def half_starts(half):
    side = lax.axis_index("pair")
    return (
        pl.multiple_of(side * half, LANES),
        pl.multiple_of((1 - side) * half, LANES),
    )


def gate_kernel(block, *refs):
    *own_refs, gate_ref, gates_ref = refs
    half = own_refs[0].shape[-1]
    units = gate_ref.shape[1]
    own_start, _ = half_starts(half)
    rows = rows_of(own_refs).astype(jnp.bfloat16)
    for start in range(0, units, block):
        part = slice(start, start + block)
        gates_ref[:, part] = jnp.dot(
            rows, gate_ref[pl.ds(own_start, half), part], preferred_element_type=jnp.float32
        )


def store_rows(offsets, target, columns, product):
    me = lax.axis_index("devs")
    rows = target.shape[1]
    for j, offset in enumerate(offsets):
        target[lax.bitwise_xor(me, offset), :, columns] = product[
            j * rows : (j + 1) * rows
        ].astype(target.dtype)


def expert_kernel(block, piece, offsets, parts, *refs):
    own_refs, refs = refs[:parts], refs[parts:]
    other_refs, refs = refs[:parts], refs[parts:]
    (
        up_ref,
        gate_ref,
        gates_ref,
        down_ref,
        meta_other_ref,
        sent_ref,
        units_ref,
        rows_ref,
    ) = refs
    width = rows_ref.shape[1]
    half = width // 2
    units = gate_ref.shape[1]
    own_start, other_start = half_starts(half)

    own, other = rows_of(own_refs), rows_of(other_refs)
    squares = jnp.sum(own * own, axis=-1, keepdims=True) + jnp.sum(
        other * other, axis=-1, keepdims=True
    )
    inv_rms = lax.rsqrt(squares / width + 1e-05)
    other = other.astype(jnp.bfloat16)
    rows_ref[:, pl.ds(own_start, half)] = own.astype(jnp.bfloat16)
    rows_ref[:, pl.ds(other_start, half)] = other

    for start in range(0, units, block):
        part = slice(start, start + block)
        gate = gates_ref[:, part] + jnp.dot(
            other, gate_ref[pl.ds(other_start, half), part], preferred_element_type=jnp.float32
        )
        gate = jax.nn.silu(gate * inv_rms) * inv_rms
        up = jnp.dot(rows_ref[...], up_ref[:, part], preferred_element_type=jnp.float32)
        units_ref[:, part] = (gate * up).astype(jnp.bfloat16)
    for start in range(0, half, piece):
        columns = pl.ds(pl.multiple_of(other_start + start, LANES), piece)
        product = jnp.dot(
            units_ref[...], down_ref[:, columns], preferred_element_type=jnp.float32
        )
        store_rows(offsets, sent_ref, slice(start, start + piece), product)


def keep_kernel(piece, offsets, units_ref, down_ref, kept_ref):
    half = kept_ref.shape[-1]
    own_start, _ = half_starts(half)
    for start in range(0, half, piece):
        columns = pl.ds(pl.multiple_of(own_start + start, LANES), piece)
        product = jnp.dot(
            units_ref[...], down_ref[:, columns], preferred_element_type=jnp.float32
        )
        store_rows(offsets, kept_ref, slice(start, start + piece), product)


def add_kernel(kept_ref, received_ref, out_ref):
    out_ref[...] = (kept_ref[...] + received_ref[...].astype(jnp.float32)).astype(jnp.bfloat16)


def combine_kernel(
    experts, returned_ref, hidden_ref, meta_ref, meta_other_ref, out_ref
):
    devices, rows, half = returned_ref.shape
    batches, per_batch, _ = out_ref.shape
    owners = devices // experts
    meta = meta_ref[...] + meta_other_ref[...]
    squares = meta[:, experts : experts + 1]
    inv_rms = lax.rsqrt(squares / (2 * half) + 1e-05)
    logits = meta * inv_rms
    chosen = meta_ref[:, experts + 1 : experts + 3].astype(jnp.int32)
    lane = lax.broadcasted_iota(jnp.int32, (rows, LANES), 1)
    first, second = chosen[:, 0:1], chosen[:, 1:2]
    logit_first = jnp.sum(jnp.where(lane == first, logits, 0.0), axis=-1, keepdims=True)
    logit_second = jnp.sum(jnp.where(lane == second, logits, 0.0), axis=-1, keepdims=True)
    gate_first = jax.nn.sigmoid(logit_first - logit_second)
    gate_second = jax.nn.sigmoid(logit_second - logit_first)
    result = hidden_ref[...].astype(jnp.float32)
    for e in range(experts):
        expert_out = returned_ref[e * owners].astype(jnp.float32)
        for o in range(1, owners):
            expert_out += returned_ref[e * owners + o].astype(jnp.float32)
        weight = jnp.where(first == e, gate_first, 0.0) + jnp.where(second == e, gate_second, 0.0)
        result += weight * expert_out
    for b in range(batches):
        out_ref[b] = result[b * per_batch : (b + 1) * per_batch].astype(jnp.bfloat16)


VMEM = pl.BlockSpec(memory_space=pltpu.VMEM)
HBM = pl.BlockSpec(memory_space=pltpu.HBM)


def far(array):
    return pltpu.with_memory_space_constraint(array, pltpu.HBM)


def near(array):
    return pltpu.with_memory_space_constraint(array, pltpu.VMEM)


def fetch(meta, after, *wanted):
    near = [
        jax.ShapeDtypeStruct((count, weights.shape[1]), weights.dtype)
        for weights, _, count in wanted
    ]
    *loaded, meta = pl.pallas_call(
        functools.partial(fetch_kernel, [start for _, start, _ in wanted]),
        in_specs=[VMEM, VMEM] + [HBM] * len(wanted),
        out_specs=[VMEM] * (len(wanted) + 1),
        out_shape=near + [jax.ShapeDtypeStruct(meta.shape, meta.dtype)],
        scratch_shapes=[pltpu.SemaphoreType.DMA((len(wanted),))],
        compiler_params=pltpu.CompilerParams(vmem_limit_bytes=1 << 20),
        cost_estimate=pl.CostEstimate(
            flops=0, bytes_accessed=2 * sum(array.size for array in near), transcendentals=0
        ),
    )(after, meta, *[far(weights) for weights, _, _ in wanted])
    return loaded, meta


def swap_devices(value, offset, devices):
    return lax.ppermute(value, "devs", [(d, d ^ offset) for d in range(devices)])


def swap_cores(value):
    return lax.ppermute(value, "pair", [(0, 1), (1, 0)])


def on_device(
    query, key_cache, value_cache, lengths, residual, router, routes, w_gate, w_up, w_down
):
    devices = lax.axis_size("devs")
    experts = router.shape[1]
    batches, per_batch, half = query.shape
    rows = batches * per_batch
    inputs = (
        query,
        key_cache,
        value_cache,
        lengths,
        residual,
        jnp.transpose(router),
        jnp.transpose(routes, (0, 2, 1)),
    )
    width, units = w_gate.shape
    block = min(512, units)
    piece = min(512, half)
    count = devices * rows
    owners = devices // experts
    hidden, meta = pl.pallas_call(
        attend_kernel,
        in_specs=[HBM] * 7,
        out_specs=[VMEM] * 2,
        out_shape=[
            jax.ShapeDtypeStruct((rows, half), jnp.bfloat16),
            jax.ShapeDtypeStruct((rows, LANES), jnp.float32),
        ],
        scratch_shapes=[
            (pltpu.SMEM if array.dtype == jnp.int32 else pltpu.VMEM)(array.shape, array.dtype)
            for array in inputs
        ]
        + [pltpu.SemaphoreType.DMA((7,))],
        compiler_params=pltpu.CompilerParams(vmem_limit_bytes=16 << 20),
    )(*[far(array) for array in inputs])

    offsets = [k * owners for k in range(experts)]
    crossed = [swap_devices(hidden, offset, devices) for offset in offsets[1:]]
    (up_near,), meta = fetch(meta, meta, (w_up, 0, width))
    held = [
        pl.pallas_call(
            stack_kernel,
            in_specs=[VMEM] * (experts + 1),
            out_specs=VMEM,
            out_shape=jax.ShapeDtypeStruct((experts, rows, half), jnp.bfloat16),
            compiler_params=pltpu.CompilerParams(vmem_limit_bytes=2 << 20),
        )(hidden, *crossed, meta)
    ]
    step = 1
    while step < owners:
        if len(held) > 1:
            held = [jnp.concatenate(held, axis=0)]
        held.append(swap_devices(held[0], step, devices))
        offsets += [offset ^ step for offset in offsets]
        step *= 2
    others = [swap_cores(held[0])]
    if len(held) > 1:
        others.append(swap_cores(held[1]))
    meta_other = swap_cores(meta)
    parts = len(held)
    w_gate, w_up, w_down = near(w_gate), up_near, near(w_down)
    gates = pl.pallas_call(
        functools.partial(gate_kernel, block),
        in_specs=[VMEM] * (parts + 1),
        out_specs=VMEM,
        out_shape=jax.ShapeDtypeStruct((count, units), jnp.float32),
        compiler_params=pltpu.CompilerParams(vmem_limit_bytes=min(48, count // 16) << 20),
        cost_estimate=pl.CostEstimate(
            flops=2 * count * half * units, bytes_accessed=2 * half * units, transcendentals=0
        ),
    )(*held, w_gate)
    sent, units_bf = pl.pallas_call(
        functools.partial(expert_kernel, block, piece, offsets, parts),
        in_specs=[VMEM] * (2 * parts + 5),
        out_specs=[VMEM] * 2,
        out_shape=[
            jax.ShapeDtypeStruct((devices, rows, half), jnp.bfloat16),
            jax.ShapeDtypeStruct((count, units), jnp.bfloat16),
        ],
        scratch_shapes=[pltpu.VMEM((count, width), jnp.bfloat16)],
        compiler_params=pltpu.CompilerParams(vmem_limit_bytes=min(48, count // 8) << 20),
    )(*held, *others, w_up, w_gate, gates, w_down, meta_other)
    received = swap_cores(sent)
    kept = pl.pallas_call(
        functools.partial(keep_kernel, piece, offsets),
        in_specs=[VMEM] * 2,
        out_specs=VMEM,
        out_shape=jax.ShapeDtypeStruct((devices, rows, half), jnp.float32),
        compiler_params=pltpu.CompilerParams(vmem_limit_bytes=min(48, count // 16) << 20),
        cost_estimate=pl.CostEstimate(
            flops=2 * count * half * units, bytes_accessed=2 * half * units, transcendentals=0
        ),
    )(units_bf, w_down)
    summed = pl.pallas_call(
        add_kernel,
        in_specs=[VMEM] * 2,
        out_specs=VMEM,
        out_shape=jax.ShapeDtypeStruct((devices, rows, half), jnp.bfloat16),
        compiler_params=pltpu.CompilerParams(vmem_limit_bytes=min(48, count // 16) << 20),
    )(kept, received)
    returned = lax.all_to_all(summed, "devs", split_axis=0, concat_axis=0, tiled=True)
    return pl.pallas_call(
        functools.partial(combine_kernel, experts),
        in_specs=[VMEM] * 4,
        out_specs=VMEM,
        out_shape=jax.ShapeDtypeStruct(query.shape, jnp.bfloat16),
        compiler_params=pltpu.CompilerParams(vmem_limit_bytes=16 << 20),
    )(returned, hidden, meta, meta_other)


def solution(mesh):
    in_specs = (
        P(None, ("groups", "devs"), "pair"),
        P(None, ("groups", "devs"), None, "pair"),
        P(None, ("groups", "devs"), None, "pair"),
        P(None, ("groups", "devs")),
        P(None, ("groups", "devs"), "pair"),
        P("pair", None),
        P(None, ("groups", "devs"), None),
        P(None, ("devs", "pair")),
        P(None, ("devs", "pair")),
        P(("devs", "pair"), None),
    )
    out_specs = P(None, ("groups", "devs"), "pair")
    return jax.shard_map(
        on_device, mesh=mesh, in_specs=in_specs, out_specs=out_specs, check_vma=False
    )
```

```python
import functools
import math

import jax
import jax.numpy as jnp
from jax import lax
from jax.experimental import pallas as pl
from jax.experimental.pallas import tpu as pltpu
from jax.sharding import PartitionSpec as P

HD = 128
LANES = 128


def attend_kernel(
    query_hbm,
    key_hbm,
    value_hbm,
    lengths_hbm,
    residual_hbm,
    router_hbm,
    routes_hbm,
    hidden_ref,
    meta_ref,
    query_ref,
    key_ref,
    value_ref,
    lengths_ref,
    residual_ref,
    router_ref,
    routes_ref,
    arrival,
):
    batches, per_batch, width = query_ref.shape
    rows = batches * per_batch
    cache_len = key_ref.shape[2]
    kv_local = key_ref.shape[3] // HD
    group = width // key_ref.shape[3]
    early = [(query_hbm, query_ref), (lengths_hbm, lengths_ref), (key_hbm, key_ref)]
    late = [
        (value_hbm, value_ref),
        (residual_hbm, residual_ref),
        (router_hbm, router_ref),
        (routes_hbm, routes_ref),
    ]
    copies = [
        pltpu.make_async_copy(source, target, arrival.at[i])
        for i, (source, target) in enumerate(early + late)
    ]
    for copy in copies:
        copy.start()
    for copy in copies[: len(early)]:
        copy.wait()

    def stacked(ref):
        return jnp.concatenate([ref[b].astype(jnp.float32) for b in range(batches)], axis=0)

    queries = stacked(query_ref)
    tall = group * rows
    row_of = lax.rem(lax.broadcasted_iota(jnp.int32, (tall, 1), 0), rows)
    position = lax.broadcasted_iota(jnp.int32, (tall, cache_len), 1)
    limit = jnp.zeros((tall, 1), jnp.int32)
    for r in range(rows):
        limit = jnp.where(row_of == r, lengths_ref[r // per_batch, r % per_batch], limit)
    live = position < limit
    pieces = []
    for k in range(kv_local):
        heads = jnp.concatenate(
            [queries[:, (k * group + j) * HD : (k * group + j + 1) * HD] for j in range(group)],
            axis=0,
        ).astype(jnp.bfloat16)
        columns = slice(k * HD, (k + 1) * HD)
        scores = jnp.zeros((tall, cache_len), jnp.float32)
        for r in range(rows):
            keys = key_ref[r // per_batch, r % per_batch, :, columns]
            part = lax.dot_general(
                heads, keys, (((1,), (1,)), ((), ())), preferred_element_type=jnp.float32
            )
            scores = jnp.where(row_of == r, part, scores)
        scores = jnp.where(live, scores * (1.0 / math.sqrt(HD)), -jnp.inf)
        peak = jnp.max(scores, axis=-1, keepdims=True)
        weights = jnp.where(live, jnp.exp(scores - peak), 0.0)
        total = jnp.sum(weights, axis=-1, keepdims=True)
        weights_bf = weights.astype(jnp.bfloat16)
        if k == 0:
            for copy in copies[len(early) :]:
                copy.wait()
        mixed = jnp.zeros((tall, HD), jnp.float32)
        for r in range(rows):
            values = value_ref[r // per_batch, r % per_batch, :, columns]
            part = jnp.dot(weights_bf, values, preferred_element_type=jnp.float32)
            mixed = jnp.where(row_of == r, part, mixed)
        mixed = mixed / total
        pieces += [mixed[j * rows : (j + 1) * rows] for j in range(group)]
    attended = jnp.concatenate(pieces, axis=1)
    hidden = (stacked(residual_ref) + attended).astype(jnp.bfloat16)
    wide = hidden.astype(jnp.float32)
    logits = lax.dot_general(
        hidden, router_ref[...], (((1,), (1,)), ((), ())), preferred_element_type=jnp.float32
    )
    squares = jnp.sum(wide * wide, axis=-1, keepdims=True)
    experts = router_ref.shape[0]
    row = lax.broadcasted_iota(jnp.int32, (rows, 1), 0)
    meta_ref[...] = jnp.zeros_like(meta_ref)
    meta_ref[:, :experts] = logits
    meta_ref[:, experts : experts + 1] = squares
    for which in range(2):
        route = jnp.zeros((rows, 1), jnp.int32)
        for r in range(rows):
            route = jnp.where(row == r, routes_ref[r // per_batch, which, r % per_batch], route)
        lane = experts + 1 + which
        meta_ref[:, lane : lane + 1] = route.astype(jnp.float32)
    hidden_ref[...] = hidden


def fetch_kernel(starts, after_ref, meta_ref, *refs):
    count = len(starts)
    sources, targets, meta_out_ref, arrival = (
        refs[:count],
        refs[count : 2 * count],
        refs[2 * count],
        refs[2 * count + 1],
    )
    copies = [
        pltpu.make_async_copy(
            source.at[pl.ds(start, target.shape[0])], target, arrival.at[i]
        )
        for i, (start, source, target) in enumerate(zip(starts, sources, targets))
    ]
    for copy in copies:
        copy.start()
    meta_out_ref[...] = meta_ref[...]
    for copy in copies:
        copy.wait()


def stack_kernel(*refs):
    for i, ref in enumerate(refs[:-3]):
        refs[-1][i] = ref[...]


def rows_of(refs):
    half = refs[0].shape[-1]
    tall = [ref[...].astype(jnp.float32).reshape(-1, half) for ref in refs]
    return jnp.concatenate(tall, axis=0)


def half_starts(half):
    side = lax.axis_index("pair")
    return (
        pl.multiple_of(side * half, LANES),
        pl.multiple_of((1 - side) * half, LANES),
    )


def gate_kernel(block, *refs):
    *own_refs, gate_ref, gates_ref = refs
    half = own_refs[0].shape[-1]
    units = gate_ref.shape[1]
    own_start, _ = half_starts(half)
    rows = rows_of(own_refs).astype(jnp.bfloat16)
    for start in range(0, units, block):
        part = slice(start, start + block)
        gates_ref[:, part] = jnp.dot(
            rows, gate_ref[pl.ds(own_start, half), part], preferred_element_type=jnp.float32
        )


def store_rows(offsets, target, columns, product):
    me = lax.axis_index("devs")
    rows = target.shape[1]
    for j, offset in enumerate(offsets):
        target[lax.bitwise_xor(me, offset), :, columns] = product[
            j * rows : (j + 1) * rows
        ].astype(target.dtype)


def expert_kernel(block, parts, *refs):
    own_refs, refs = refs[:parts], refs[parts:]
    other_refs, refs = refs[:parts], refs[parts:]
    (
        up_ref,
        gate_ref,
        gates_ref,
        meta_other_ref,
        units_ref,
        rows_ref,
    ) = refs
    width = rows_ref.shape[1]
    half = width // 2
    units = gate_ref.shape[1]
    own_start, other_start = half_starts(half)

    own, other = rows_of(own_refs), rows_of(other_refs)
    squares = jnp.sum(own * own, axis=-1, keepdims=True) + jnp.sum(
        other * other, axis=-1, keepdims=True
    )
    inv_rms = lax.rsqrt(squares / width + 1e-05)
    other = other.astype(jnp.bfloat16)
    rows_ref[:, pl.ds(own_start, half)] = own.astype(jnp.bfloat16)
    rows_ref[:, pl.ds(other_start, half)] = other

    for start in range(0, units, block):
        part = slice(start, start + block)
        gate = gates_ref[:, part] + jnp.dot(
            other, gate_ref[pl.ds(other_start, half), part], preferred_element_type=jnp.float32
        )
        gate = jax.nn.silu(gate * inv_rms) * inv_rms
        up = jnp.dot(rows_ref[...], up_ref[:, part], preferred_element_type=jnp.float32)
        units_ref[:, part] = (gate * up).astype(jnp.bfloat16)


def down_kernel(piece, offsets, own, units_ref, down_ref, out_ref):
    half = out_ref.shape[-1]
    base = half_starts(half)[0 if own else 1]
    for start in range(0, half, piece):
        columns = pl.ds(pl.multiple_of(base + start, LANES), piece)
        product = jnp.dot(
            units_ref[...], down_ref[:, columns], preferred_element_type=jnp.float32
        )
        store_rows(offsets, out_ref, slice(start, start + piece), product)


def add_kernel(kept_ref, received_ref, out_ref):
    out_ref[...] = (kept_ref[...] + received_ref[...].astype(jnp.float32)).astype(jnp.bfloat16)


def combine_kernel(
    experts, returned_ref, hidden_ref, meta_ref, meta_other_ref, out_ref
):
    devices, rows, half = returned_ref.shape
    batches, per_batch, _ = out_ref.shape
    owners = devices // experts
    meta = meta_ref[...] + meta_other_ref[...]
    squares = meta[:, experts : experts + 1]
    inv_rms = lax.rsqrt(squares / (2 * half) + 1e-05)
    logits = meta * inv_rms
    chosen = meta_ref[:, experts + 1 : experts + 3].astype(jnp.int32)
    lane = lax.broadcasted_iota(jnp.int32, (rows, LANES), 1)
    first, second = chosen[:, 0:1], chosen[:, 1:2]
    logit_first = jnp.sum(jnp.where(lane == first, logits, 0.0), axis=-1, keepdims=True)
    logit_second = jnp.sum(jnp.where(lane == second, logits, 0.0), axis=-1, keepdims=True)
    gate_first = jax.nn.sigmoid(logit_first - logit_second)
    gate_second = jax.nn.sigmoid(logit_second - logit_first)
    result = hidden_ref[...].astype(jnp.float32)
    for e in range(experts):
        expert_out = returned_ref[e * owners].astype(jnp.float32)
        for o in range(1, owners):
            expert_out += returned_ref[e * owners + o].astype(jnp.float32)
        weight = jnp.where(first == e, gate_first, 0.0) + jnp.where(second == e, gate_second, 0.0)
        result += weight * expert_out
    for b in range(batches):
        out_ref[b] = result[b * per_batch : (b + 1) * per_batch].astype(jnp.bfloat16)


VMEM = pl.BlockSpec(memory_space=pltpu.VMEM)
HBM = pl.BlockSpec(memory_space=pltpu.HBM)


def far(array):
    return pltpu.with_memory_space_constraint(array, pltpu.HBM)


def near(array):
    return pltpu.with_memory_space_constraint(array, pltpu.VMEM)


def fetch(meta, after, *wanted):
    near = [
        jax.ShapeDtypeStruct((count, weights.shape[1]), weights.dtype)
        for weights, _, count in wanted
    ]
    *loaded, meta = pl.pallas_call(
        functools.partial(fetch_kernel, [start for _, start, _ in wanted]),
        in_specs=[VMEM, VMEM] + [HBM] * len(wanted),
        out_specs=[VMEM] * (len(wanted) + 1),
        out_shape=near + [jax.ShapeDtypeStruct(meta.shape, meta.dtype)],
        scratch_shapes=[pltpu.SemaphoreType.DMA((len(wanted),))],
        compiler_params=pltpu.CompilerParams(vmem_limit_bytes=1 << 20),
        cost_estimate=pl.CostEstimate(
            flops=0, bytes_accessed=2 * sum(array.size for array in near), transcendentals=0
        ),
    )(after, meta, *[far(weights) for weights, _, _ in wanted])
    return loaded, meta


def swap_devices(value, offset, devices):
    return lax.ppermute(value, "devs", [(d, d ^ offset) for d in range(devices)])


def swap_cores(value):
    return lax.ppermute(value, "pair", [(0, 1), (1, 0)])


def on_device(
    query, key_cache, value_cache, lengths, residual, router, routes, w_gate, w_up, w_down
):
    devices = lax.axis_size("devs")
    experts = router.shape[1]
    batches, per_batch, half = query.shape
    rows = batches * per_batch
    inputs = (
        query,
        key_cache,
        value_cache,
        lengths,
        residual,
        jnp.transpose(router),
        jnp.transpose(routes, (0, 2, 1)),
    )
    width, units = w_gate.shape
    block = min(512, units)
    piece = min(512, half)
    count = devices * rows
    owners = devices // experts
    hidden, meta = pl.pallas_call(
        attend_kernel,
        in_specs=[HBM] * 7,
        out_specs=[VMEM] * 2,
        out_shape=[
            jax.ShapeDtypeStruct((rows, half), jnp.bfloat16),
            jax.ShapeDtypeStruct((rows, LANES), jnp.float32),
        ],
        scratch_shapes=[
            (pltpu.SMEM if array.dtype == jnp.int32 else pltpu.VMEM)(array.shape, array.dtype)
            for array in inputs
        ]
        + [pltpu.SemaphoreType.DMA((7,))],
        compiler_params=pltpu.CompilerParams(vmem_limit_bytes=6 << 20),
    )(*[far(array) for array in inputs])

    offsets = [k * owners for k in range(experts)]
    crossed = [swap_devices(hidden, offset, devices) for offset in offsets[1:]]
    _, meta = fetch(meta, meta, (w_up, 0, 16))
    w_gate, w_up, w_down = near(w_gate), near(w_up), near(w_down)
    held = [
        pl.pallas_call(
            stack_kernel,
            in_specs=[VMEM] * (experts + 2),
            out_specs=VMEM,
            out_shape=jax.ShapeDtypeStruct((experts, rows, half), jnp.bfloat16),
            compiler_params=pltpu.CompilerParams(vmem_limit_bytes=2 << 20),
        )(hidden, *crossed, meta, w_gate)
    ]
    step = 1
    while step < owners:
        if len(held) > 1:
            held = [jnp.concatenate(held, axis=0)]
        held.append(swap_devices(held[0], step, devices))
        offsets += [offset ^ step for offset in offsets]
        step *= 2
    others = [swap_cores(held[0])]
    if len(held) > 1:
        others.append(swap_cores(held[1]))
    meta_other = swap_cores(meta)
    parts = len(held)
    gates = pl.pallas_call(
        functools.partial(gate_kernel, block),
        in_specs=[VMEM] * (parts + 1),
        out_specs=VMEM,
        out_shape=jax.ShapeDtypeStruct((count, units), jnp.float32),
        compiler_params=pltpu.CompilerParams(vmem_limit_bytes=min(48, count // 16) << 20),
        cost_estimate=pl.CostEstimate(
            flops=2 * count * half * units, bytes_accessed=2 * half * units, transcendentals=0
        ),
    )(*held, w_gate)
    units_bf = pl.pallas_call(
        functools.partial(expert_kernel, block, parts),
        in_specs=[VMEM] * (2 * parts + 4),
        out_specs=VMEM,
        out_shape=jax.ShapeDtypeStruct((count, units), jnp.bfloat16),
        scratch_shapes=[pltpu.VMEM((count, width), jnp.bfloat16)],
        compiler_params=pltpu.CompilerParams(vmem_limit_bytes=min(48, count // 8) << 20),
    )(*held, *others, w_up, w_gate, gates, meta_other)

    def project(own, dtype):
        return pl.pallas_call(
            functools.partial(down_kernel, piece, offsets, own),
            in_specs=[VMEM] * 2,
            out_specs=VMEM,
            out_shape=jax.ShapeDtypeStruct((devices, rows, half), dtype),
            compiler_params=pltpu.CompilerParams(vmem_limit_bytes=min(48, count // 16) << 20),
            cost_estimate=pl.CostEstimate(
                flops=2 * count * half * units,
                bytes_accessed=2 * half * units,
                transcendentals=0,
            ),
        )(units_bf, w_down)

    received = swap_cores(project(False, jnp.bfloat16))
    kept = project(True, jnp.float32)
    summed = pl.pallas_call(
        add_kernel,
        in_specs=[VMEM] * 2,
        out_specs=VMEM,
        out_shape=jax.ShapeDtypeStruct((devices, rows, half), jnp.bfloat16),
        compiler_params=pltpu.CompilerParams(vmem_limit_bytes=min(48, count // 16) << 20),
    )(kept, received)
    returned = lax.all_to_all(summed, "devs", split_axis=0, concat_axis=0, tiled=True)
    return pl.pallas_call(
        functools.partial(combine_kernel, experts),
        in_specs=[VMEM] * 4,
        out_specs=VMEM,
        out_shape=jax.ShapeDtypeStruct(query.shape, jnp.bfloat16),
        compiler_params=pltpu.CompilerParams(vmem_limit_bytes=6 << 20),
    )(returned, hidden, meta, meta_other)


def solution(mesh):
    in_specs = (
        P(None, ("groups", "devs"), "pair"),
        P(None, ("groups", "devs"), None, "pair"),
        P(None, ("groups", "devs"), None, "pair"),
        P(None, ("groups", "devs")),
        P(None, ("groups", "devs"), "pair"),
        P("pair", None),
        P(None, ("groups", "devs"), None),
        P(None, ("devs", "pair")),
        P(None, ("devs", "pair")),
        P(("devs", "pair"), None),
    )
    out_specs = P(None, ("groups", "devs"), "pair")
    return jax.shard_map(
        on_device, mesh=mesh, in_specs=in_specs, out_specs=out_specs, check_vma=False
    )
```

```python
import functools
import math

import jax
import jax.numpy as jnp
from jax import lax
from jax.experimental import pallas as pl
from jax.experimental.pallas import tpu as pltpu
from jax.sharding import PartitionSpec as P

HD = 128
LANES = 128


def attend_kernel(
    query_hbm,
    key_hbm,
    value_hbm,
    lengths_hbm,
    residual_hbm,
    router_hbm,
    routes_hbm,
    hidden_ref,
    meta_ref,
    query_ref,
    key_ref,
    value_ref,
    lengths_ref,
    residual_ref,
    router_ref,
    routes_ref,
    arrival,
):
    batches, per_batch, width = query_ref.shape
    rows = batches * per_batch
    cache_len = key_ref.shape[2]
    kv_local = key_ref.shape[3] // HD
    group = width // key_ref.shape[3]
    early = [(query_hbm, query_ref), (lengths_hbm, lengths_ref), (key_hbm, key_ref)]
    late = [
        (value_hbm, value_ref),
        (residual_hbm, residual_ref),
        (router_hbm, router_ref),
        (routes_hbm, routes_ref),
    ]
    copies = [
        pltpu.make_async_copy(source, target, arrival.at[i])
        for i, (source, target) in enumerate(early + late)
    ]
    for copy in copies:
        copy.start()
    for copy in copies[: len(early)]:
        copy.wait()

    def stacked(ref):
        return jnp.concatenate([ref[b].astype(jnp.float32) for b in range(batches)], axis=0)

    queries = stacked(query_ref)
    tall = group * rows
    row_of = lax.rem(lax.broadcasted_iota(jnp.int32, (tall, 1), 0), rows)
    position = lax.broadcasted_iota(jnp.int32, (tall, cache_len), 1)
    limit = jnp.zeros((tall, 1), jnp.int32)
    for r in range(rows):
        limit = jnp.where(row_of == r, lengths_ref[r // per_batch, r % per_batch], limit)
    live = position < limit
    pieces, all_scores = [], []
    for k in range(kv_local):
        heads = jnp.concatenate(
            [queries[:, (k * group + j) * HD : (k * group + j + 1) * HD] for j in range(group)],
            axis=0,
        ).astype(jnp.bfloat16)
        columns = slice(k * HD, (k + 1) * HD)
        scores = jnp.zeros((tall, cache_len), jnp.float32)
        for r in range(rows):
            keys = key_ref[r // per_batch, r % per_batch, :, columns]
            part = lax.dot_general(
                heads, keys, (((1,), (1,)), ((), ())), preferred_element_type=jnp.float32
            )
            scores = jnp.where(row_of == r, part, scores)
        all_scores.append(scores)
    for copy in copies[len(early) :]:
        copy.wait()
    for k, scores in enumerate(all_scores):
        columns = slice(k * HD, (k + 1) * HD)
        scores = jnp.where(live, scores * (1.0 / math.sqrt(HD)), -jnp.inf)
        peak = jnp.max(scores, axis=-1, keepdims=True)
        weights = jnp.where(live, jnp.exp(scores - peak), 0.0)
        total = jnp.sum(weights, axis=-1, keepdims=True)
        weights_bf = weights.astype(jnp.bfloat16)
        mixed = jnp.zeros((tall, HD), jnp.float32)
        for r in range(rows):
            values = value_ref[r // per_batch, r % per_batch, :, columns]
            part = jnp.dot(weights_bf, values, preferred_element_type=jnp.float32)
            mixed = jnp.where(row_of == r, part, mixed)
        mixed = mixed / total
        pieces += [mixed[j * rows : (j + 1) * rows] for j in range(group)]
    attended = jnp.concatenate(pieces, axis=1)
    hidden = (stacked(residual_ref) + attended).astype(jnp.bfloat16)
    wide = hidden.astype(jnp.float32)
    logits = lax.dot_general(
        hidden, router_ref[...], (((1,), (1,)), ((), ())), preferred_element_type=jnp.float32
    )
    squares = jnp.sum(wide * wide, axis=-1, keepdims=True)
    experts = router_ref.shape[0]
    row = lax.broadcasted_iota(jnp.int32, (rows, 1), 0)
    meta_ref[...] = jnp.zeros_like(meta_ref)
    meta_ref[:, :experts] = logits
    meta_ref[:, experts : experts + 1] = squares
    for which in range(2):
        route = jnp.zeros((rows, 1), jnp.int32)
        for r in range(rows):
            route = jnp.where(row == r, routes_ref[r // per_batch, which, r % per_batch], route)
        lane = experts + 1 + which
        meta_ref[:, lane : lane + 1] = route.astype(jnp.float32)
    hidden_ref[...] = hidden


def fetch_kernel(starts, after_ref, meta_ref, *refs):
    count = len(starts)
    sources, targets, meta_out_ref, arrival = (
        refs[:count],
        refs[count : 2 * count],
        refs[2 * count],
        refs[2 * count + 1],
    )
    copies = [
        pltpu.make_async_copy(
            source.at[pl.ds(start, target.shape[0])], target, arrival.at[i]
        )
        for i, (start, source, target) in enumerate(zip(starts, sources, targets))
    ]
    for copy in copies:
        copy.start()
    meta_out_ref[...] = meta_ref[...]
    for copy in copies:
        copy.wait()


def stack_kernel(*refs):
    for i, ref in enumerate(refs[:-3]):
        refs[-1][i] = ref[...]


def rows_of(refs):
    half = refs[0].shape[-1]
    tall = [ref[...].astype(jnp.float32).reshape(-1, half) for ref in refs]
    return jnp.concatenate(tall, axis=0)


def half_starts(half):
    side = lax.axis_index("pair")
    return (
        pl.multiple_of(side * half, LANES),
        pl.multiple_of((1 - side) * half, LANES),
    )


def gate_kernel(block, *refs):
    *own_refs, gate_ref, gates_ref = refs
    half = own_refs[0].shape[-1]
    units = gate_ref.shape[1]
    own_start, _ = half_starts(half)
    rows = rows_of(own_refs).astype(jnp.bfloat16)
    for start in range(0, units, block):
        part = slice(start, start + block)
        gates_ref[:, part] = jnp.dot(
            rows, gate_ref[pl.ds(own_start, half), part], preferred_element_type=jnp.float32
        )


def store_rows(offsets, target, columns, product):
    me = lax.axis_index("devs")
    rows = target.shape[1]
    for j, offset in enumerate(offsets):
        target[lax.bitwise_xor(me, offset), :, columns] = product[
            j * rows : (j + 1) * rows
        ].astype(target.dtype)


def expert_kernel(block, experts, parts, *refs):
    own_refs, refs = refs[:parts], refs[parts:]
    other_refs, refs = refs[:parts], refs[parts:]
    (
        up_ref,
        gate_ref,
        gates_ref,
        meta_ref,
        meta_other_ref,
        units_ref,
        weights_ref,
        rows_ref,
    ) = refs
    width = rows_ref.shape[1]
    half = width // 2
    units = gate_ref.shape[1]
    own_start, other_start = half_starts(half)

    own, other = rows_of(own_refs), rows_of(other_refs)
    squares = jnp.sum(own * own, axis=-1, keepdims=True) + jnp.sum(
        other * other, axis=-1, keepdims=True
    )
    inv_rms = lax.rsqrt(squares / width + 1e-05)
    other = other.astype(jnp.bfloat16)
    rows_ref[:, pl.ds(own_start, half)] = own.astype(jnp.bfloat16)
    rows_ref[:, pl.ds(other_start, half)] = other

    for start in range(0, units, block):
        part = slice(start, start + block)
        gate = gates_ref[:, part] + jnp.dot(
            other, gate_ref[pl.ds(other_start, half), part], preferred_element_type=jnp.float32
        )
        gate = jax.nn.silu(gate * inv_rms) * inv_rms
        up = jnp.dot(rows_ref[...], up_ref[:, part], preferred_element_type=jnp.float32)
        units_ref[:, part] = (gate * up).astype(jnp.bfloat16)

    meta = meta_ref[...] + meta_other_ref[...]
    logits = meta * lax.rsqrt(meta[:, experts : experts + 1] / width + 1e-05)
    chosen = meta_ref[:, experts + 1 : experts + 3].astype(jnp.int32)
    first, second = chosen[:, 0:1], chosen[:, 1:2]
    lane = lax.broadcasted_iota(jnp.int32, meta.shape, 1)
    logit_first = jnp.sum(jnp.where(lane == first, logits, 0.0), axis=-1, keepdims=True)
    logit_second = jnp.sum(jnp.where(lane == second, logits, 0.0), axis=-1, keepdims=True)
    weights_ref[...] = jnp.where(
        lane == first, jax.nn.sigmoid(logit_first - logit_second), 0.0
    ) + jnp.where(lane == second, jax.nn.sigmoid(logit_second - logit_first), 0.0)


def down_kernel(piece, offsets, own, units_ref, down_ref, out_ref):
    half = out_ref.shape[-1]
    base = half_starts(half)[0 if own else 1]
    for start in range(0, half, piece):
        columns = pl.ds(pl.multiple_of(base + start, LANES), piece)
        product = jnp.dot(
            units_ref[...], down_ref[:, columns], preferred_element_type=jnp.float32
        )
        store_rows(offsets, out_ref, slice(start, start + piece), product)


def add_kernel(kept_ref, received_ref, out_ref):
    out_ref[...] = (kept_ref[...] + received_ref[...].astype(jnp.float32)).astype(jnp.bfloat16)


def combine_kernel(experts, returned_ref, hidden_ref, weights_ref, out_ref):
    devices = returned_ref.shape[0]
    batches, per_batch, _ = out_ref.shape
    owners = devices // experts
    result = hidden_ref[...].astype(jnp.float32)
    for e in range(experts):
        expert_out = returned_ref[e * owners].astype(jnp.float32)
        for o in range(1, owners):
            expert_out += returned_ref[e * owners + o].astype(jnp.float32)
        result += weights_ref[:, e : e + 1] * expert_out
    for b in range(batches):
        out_ref[b] = result[b * per_batch : (b + 1) * per_batch].astype(jnp.bfloat16)


VMEM = pl.BlockSpec(memory_space=pltpu.VMEM)
HBM = pl.BlockSpec(memory_space=pltpu.HBM)


def far(array):
    return pltpu.with_memory_space_constraint(array, pltpu.HBM)


def near(array):
    return pltpu.with_memory_space_constraint(array, pltpu.VMEM)


def fetch(meta, after, *wanted):
    near = [
        jax.ShapeDtypeStruct((count, weights.shape[1]), weights.dtype)
        for weights, _, count in wanted
    ]
    *loaded, meta = pl.pallas_call(
        functools.partial(fetch_kernel, [start for _, start, _ in wanted]),
        in_specs=[VMEM, VMEM] + [HBM] * len(wanted),
        out_specs=[VMEM] * (len(wanted) + 1),
        out_shape=near + [jax.ShapeDtypeStruct(meta.shape, meta.dtype)],
        scratch_shapes=[pltpu.SemaphoreType.DMA((len(wanted),))],
        compiler_params=pltpu.CompilerParams(vmem_limit_bytes=1 << 20),
        cost_estimate=pl.CostEstimate(
            flops=0, bytes_accessed=2 * sum(array.size for array in near), transcendentals=0
        ),
    )(after, meta, *[far(weights) for weights, _, _ in wanted])
    return loaded, meta


def swap_devices(value, offset, devices):
    return lax.ppermute(value, "devs", [(d, d ^ offset) for d in range(devices)])


def swap_cores(value):
    return lax.ppermute(value, "pair", [(0, 1), (1, 0)])


def on_device(
    query, key_cache, value_cache, lengths, residual, router, routes, w_gate, w_up, w_down
):
    devices = lax.axis_size("devs")
    experts = router.shape[1]
    batches, per_batch, half = query.shape
    rows = batches * per_batch
    inputs = (
        query,
        key_cache,
        value_cache,
        lengths,
        residual,
        jnp.transpose(router),
        jnp.transpose(routes, (0, 2, 1)),
    )
    width, units = w_gate.shape
    block = min(512, units)
    piece = min(512, half)
    count = devices * rows
    owners = devices // experts
    hidden, meta = pl.pallas_call(
        attend_kernel,
        in_specs=[HBM] * 7,
        out_specs=[VMEM] * 2,
        out_shape=[
            jax.ShapeDtypeStruct((rows, half), jnp.bfloat16),
            jax.ShapeDtypeStruct((rows, LANES), jnp.float32),
        ],
        scratch_shapes=[
            (pltpu.SMEM if array.dtype == jnp.int32 else pltpu.VMEM)(array.shape, array.dtype)
            for array in inputs
        ]
        + [pltpu.SemaphoreType.DMA((7,))],
        compiler_params=pltpu.CompilerParams(vmem_limit_bytes=6 << 20),
    )(*[far(array) for array in inputs])

    offsets = [k * owners for k in range(experts)]
    crossed = [swap_devices(hidden, offset, devices) for offset in offsets[1:]]
    _, meta = fetch(meta, meta, (w_up, 0, 16))
    w_gate, w_up, w_down = near(w_gate), near(w_up), near(w_down)
    held = [
        pl.pallas_call(
            stack_kernel,
            in_specs=[VMEM] * (experts + 2),
            out_specs=VMEM,
            out_shape=jax.ShapeDtypeStruct((experts, rows, half), jnp.bfloat16),
            compiler_params=pltpu.CompilerParams(vmem_limit_bytes=2 << 20),
        )(hidden, *crossed, meta, w_gate)
    ]
    step = 1
    while step < owners:
        if len(held) > 1:
            held = [jnp.concatenate(held, axis=0)]
        held.append(swap_devices(held[0], step, devices))
        offsets += [offset ^ step for offset in offsets]
        step *= 2
    others = [swap_cores(held[0])]
    meta_other = swap_cores(meta)
    if len(held) > 1:
        held[1], meta_other = lax.optimization_barrier((held[1], meta_other))
        others.append(swap_cores(held[1]))
    parts = len(held)
    gates = pl.pallas_call(
        functools.partial(gate_kernel, block),
        in_specs=[VMEM] * (parts + 1),
        out_specs=VMEM,
        out_shape=jax.ShapeDtypeStruct((count, units), jnp.float32),
        compiler_params=pltpu.CompilerParams(vmem_limit_bytes=min(48, count // 16) << 20),
        cost_estimate=pl.CostEstimate(
            flops=2 * count * half * units, bytes_accessed=2 * half * units, transcendentals=0
        ),
    )(*held, w_gate)
    units_bf, weights = pl.pallas_call(
        functools.partial(expert_kernel, block, experts, parts),
        in_specs=[VMEM] * (2 * parts + 5),
        out_specs=[VMEM] * 2,
        out_shape=[
            jax.ShapeDtypeStruct((count, units), jnp.bfloat16),
            jax.ShapeDtypeStruct(meta.shape, jnp.float32),
        ],
        scratch_shapes=[pltpu.VMEM((count, width), jnp.bfloat16)],
        compiler_params=pltpu.CompilerParams(vmem_limit_bytes=min(48, count // 8) << 20),
    )(*held, *others, w_up, w_gate, gates, meta, meta_other)

    def project(own, dtype):
        return pl.pallas_call(
            functools.partial(down_kernel, piece, offsets, own),
            in_specs=[VMEM] * 2,
            out_specs=VMEM,
            out_shape=jax.ShapeDtypeStruct((devices, rows, half), dtype),
            compiler_params=pltpu.CompilerParams(vmem_limit_bytes=min(48, count // 16) << 20),
            cost_estimate=pl.CostEstimate(
                flops=2 * count * half * units,
                bytes_accessed=2 * half * units,
                transcendentals=0,
            ),
        )(units_bf, w_down)

    received = swap_cores(project(False, jnp.bfloat16))
    kept = project(True, jnp.float32)
    summed = pl.pallas_call(
        add_kernel,
        in_specs=[VMEM] * 2,
        out_specs=VMEM,
        out_shape=jax.ShapeDtypeStruct((devices, rows, half), jnp.bfloat16),
        compiler_params=pltpu.CompilerParams(vmem_limit_bytes=min(48, count // 16) << 20),
    )(kept, received)
    returned = lax.all_to_all(summed, "devs", split_axis=0, concat_axis=0, tiled=True)
    return pl.pallas_call(
        functools.partial(combine_kernel, experts),
        in_specs=[VMEM] * 3,
        out_specs=VMEM,
        out_shape=jax.ShapeDtypeStruct(query.shape, jnp.bfloat16),
        compiler_params=pltpu.CompilerParams(vmem_limit_bytes=6 << 20),
    )(returned, hidden, weights)


def solution(mesh):
    in_specs = (
        P(None, ("groups", "devs"), "pair"),
        P(None, ("groups", "devs"), None, "pair"),
        P(None, ("groups", "devs"), None, "pair"),
        P(None, ("groups", "devs")),
        P(None, ("groups", "devs"), "pair"),
        P("pair", None),
        P(None, ("groups", "devs"), None),
        P(None, ("devs", "pair")),
        P(None, ("devs", "pair")),
        P(("devs", "pair"), None),
    )
    out_specs = P(None, ("groups", "devs"), "pair")
    return jax.shard_map(
        on_device, mesh=mesh, in_specs=in_specs, out_specs=out_specs, check_vma=False
    )
```

```python
import functools
import math

import jax
import jax.numpy as jnp
from jax import lax
from jax.experimental import pallas as pl
from jax.experimental.pallas import tpu as pltpu
from jax.sharding import PartitionSpec as P

HD = 128
LANES = 128


def attend_kernel(
    query_hbm,
    key_hbm,
    value_hbm,
    lengths_hbm,
    residual_hbm,
    router_hbm,
    routes_hbm,
    up_hbm,
    hidden_ref,
    meta_ref,
    query_ref,
    key_ref,
    value_ref,
    lengths_ref,
    residual_ref,
    router_ref,
    routes_ref,
    up_ref,
    arrival,
):
    batches, per_batch, width = query_ref.shape
    rows = batches * per_batch
    cache_len = key_ref.shape[2]
    kv_local = key_ref.shape[3] // HD
    group = width // key_ref.shape[3]
    early = [(query_hbm, query_ref), (lengths_hbm, lengths_ref), (key_hbm, key_ref)]
    late = [
        (value_hbm, value_ref),
        (residual_hbm, residual_ref),
        (router_hbm, router_ref),
        (routes_hbm, routes_ref),
        (up_hbm.at[pl.ds(0, up_ref.shape[0])], up_ref),
    ]
    copies = [
        pltpu.make_async_copy(source, target, arrival.at[i])
        for i, (source, target) in enumerate(early + late)
    ]
    for copy in copies:
        copy.start()
    for copy in copies[: len(early)]:
        copy.wait()

    def stacked(ref):
        return jnp.concatenate([ref[b].astype(jnp.float32) for b in range(batches)], axis=0)

    queries = stacked(query_ref)
    tall = group * rows
    row_of = lax.rem(lax.broadcasted_iota(jnp.int32, (tall, 1), 0), rows)
    position = lax.broadcasted_iota(jnp.int32, (tall, cache_len), 1)
    limit = jnp.zeros((tall, 1), jnp.int32)
    for r in range(rows):
        limit = jnp.where(row_of == r, lengths_ref[r // per_batch, r % per_batch], limit)
    live = position < limit
    pieces, all_scores = [], []
    for k in range(kv_local):
        heads = jnp.concatenate(
            [queries[:, (k * group + j) * HD : (k * group + j + 1) * HD] for j in range(group)],
            axis=0,
        ).astype(jnp.bfloat16)
        columns = slice(k * HD, (k + 1) * HD)
        scores = jnp.zeros((tall, cache_len), jnp.float32)
        for r in range(rows):
            keys = key_ref[r // per_batch, r % per_batch, :, columns]
            part = lax.dot_general(
                heads, keys, (((1,), (1,)), ((), ())), preferred_element_type=jnp.float32
            )
            scores = jnp.where(row_of == r, part, scores)
        all_scores.append(scores)
    for copy in copies[len(early) :]:
        copy.wait()
    for k, scores in enumerate(all_scores):
        columns = slice(k * HD, (k + 1) * HD)
        scores = jnp.where(live, scores * (1.0 / math.sqrt(HD)), -jnp.inf)
        peak = jnp.max(scores, axis=-1, keepdims=True)
        weights = jnp.where(live, jnp.exp(scores - peak), 0.0)
        total = jnp.sum(weights, axis=-1, keepdims=True)
        weights_bf = weights.astype(jnp.bfloat16)
        mixed = jnp.zeros((tall, HD), jnp.float32)
        for r in range(rows):
            values = value_ref[r // per_batch, r % per_batch, :, columns]
            part = jnp.dot(weights_bf, values, preferred_element_type=jnp.float32)
            mixed = jnp.where(row_of == r, part, mixed)
        mixed = mixed / total
        pieces += [mixed[j * rows : (j + 1) * rows] for j in range(group)]
    attended = jnp.concatenate(pieces, axis=1)
    hidden = (stacked(residual_ref) + attended).astype(jnp.bfloat16)
    wide = hidden.astype(jnp.float32)
    logits = lax.dot_general(
        hidden, router_ref[...], (((1,), (1,)), ((), ())), preferred_element_type=jnp.float32
    )
    squares = jnp.sum(wide * wide, axis=-1, keepdims=True)
    experts = router_ref.shape[0]
    row = lax.broadcasted_iota(jnp.int32, (rows, 1), 0)
    meta_ref[...] = jnp.zeros_like(meta_ref)
    meta_ref[:, :experts] = logits
    meta_ref[:, experts : experts + 1] = squares
    for which in range(2):
        route = jnp.zeros((rows, 1), jnp.int32)
        for r in range(rows):
            route = jnp.where(row == r, routes_ref[r // per_batch, which, r % per_batch], route)
        lane = experts + 1 + which
        meta_ref[:, lane : lane + 1] = route.astype(jnp.float32)
    hidden_ref[...] = hidden


def stack_kernel(count, *refs):
    out_ref, start = refs[-1], 0
    for ref in refs[:count]:
        if ref.ndim == 2:
            out_ref[start] = ref[...]
            start += 1
        else:
            out_ref[start : start + ref.shape[0]] = ref[...]
            start += ref.shape[0]


def rows_of(refs):
    half = refs[0].shape[-1]
    tall = [ref[...].astype(jnp.float32).reshape(-1, half) for ref in refs]
    return jnp.concatenate(tall, axis=0)


def half_starts(half):
    side = lax.axis_index("pair")
    return (
        pl.multiple_of(side * half, LANES),
        pl.multiple_of((1 - side) * half, LANES),
    )


def gate_kernel(block, *refs):
    *own_refs, gate_ref, gates_ref = refs
    half = own_refs[0].shape[-1]
    units = gate_ref.shape[1]
    own_start, _ = half_starts(half)
    rows = rows_of(own_refs).astype(jnp.bfloat16)
    for start in range(0, units, block):
        part = slice(start, start + block)
        gates_ref[:, part] = jnp.dot(
            rows, gate_ref[pl.ds(own_start, half), part], preferred_element_type=jnp.float32
        )


def store_rows(offsets, target, columns, product):
    me = lax.axis_index("devs")
    rows = target.shape[1]
    for j, offset in enumerate(offsets):
        target[lax.bitwise_xor(me, offset), :, columns] = product[
            j * rows : (j + 1) * rows
        ].astype(target.dtype)


def expert_kernel(block, experts, parts, *refs):
    own_refs, refs = refs[:parts], refs[parts:]
    other_refs, refs = refs[:parts], refs[parts:]
    (
        up_ref,
        gate_ref,
        gates_ref,
        meta_ref,
        meta_other_ref,
        units_ref,
        weights_ref,
        rows_ref,
    ) = refs
    width = rows_ref.shape[1]
    half = width // 2
    units = gate_ref.shape[1]
    own_start, other_start = half_starts(half)

    own, other = rows_of(own_refs), rows_of(other_refs)
    squares = jnp.sum(own * own, axis=-1, keepdims=True) + jnp.sum(
        other * other, axis=-1, keepdims=True
    )
    inv_rms = lax.rsqrt(squares / width + 1e-05)
    other = other.astype(jnp.bfloat16)
    rows_ref[:, pl.ds(own_start, half)] = own.astype(jnp.bfloat16)
    rows_ref[:, pl.ds(other_start, half)] = other

    for start in range(0, units, block):
        part = slice(start, start + block)
        gate = gates_ref[:, part] + jnp.dot(
            other, gate_ref[pl.ds(other_start, half), part], preferred_element_type=jnp.float32
        )
        gate = jax.nn.silu(gate * inv_rms) * inv_rms
        up = jnp.dot(rows_ref[...], up_ref[:, part], preferred_element_type=jnp.float32)
        units_ref[:, part] = (gate * up).astype(jnp.bfloat16)

    meta = meta_ref[...] + meta_other_ref[...]
    logits = meta * lax.rsqrt(meta[:, experts : experts + 1] / width + 1e-05)
    chosen = meta_ref[:, experts + 1 : experts + 3].astype(jnp.int32)
    first, second = chosen[:, 0:1], chosen[:, 1:2]
    lane = lax.broadcasted_iota(jnp.int32, meta.shape, 1)
    logit_first = jnp.sum(jnp.where(lane == first, logits, 0.0), axis=-1, keepdims=True)
    logit_second = jnp.sum(jnp.where(lane == second, logits, 0.0), axis=-1, keepdims=True)
    weights_ref[...] = jnp.where(
        lane == first, jax.nn.sigmoid(logit_first - logit_second), 0.0
    ) + jnp.where(lane == second, jax.nn.sigmoid(logit_second - logit_first), 0.0)


def down_kernel(piece, offsets, own, units_ref, down_ref, out_ref):
    half = out_ref.shape[-1]
    base = half_starts(half)[0 if own else 1]
    for start in range(0, half, piece):
        columns = pl.ds(pl.multiple_of(base + start, LANES), piece)
        product = jnp.dot(
            units_ref[...], down_ref[:, columns], preferred_element_type=jnp.float32
        )
        store_rows(offsets, out_ref, slice(start, start + piece), product)


def add_kernel(kept_ref, received_ref, out_ref):
    out_ref[...] = (kept_ref[...] + received_ref[...].astype(jnp.float32)).astype(jnp.bfloat16)


def combine_kernel(experts, returned_ref, hidden_ref, weights_ref, out_ref):
    devices = returned_ref.shape[0]
    batches, per_batch, _ = out_ref.shape
    owners = devices // experts
    result = hidden_ref[...].astype(jnp.float32)
    for e in range(experts):
        expert_out = returned_ref[e * owners].astype(jnp.float32)
        for o in range(1, owners):
            expert_out += returned_ref[e * owners + o].astype(jnp.float32)
        result += weights_ref[:, e : e + 1] * expert_out
    for b in range(batches):
        out_ref[b] = result[b * per_batch : (b + 1) * per_batch].astype(jnp.bfloat16)


VMEM = pl.BlockSpec(memory_space=pltpu.VMEM)
HBM = pl.BlockSpec(memory_space=pltpu.HBM)


def far(array):
    return pltpu.with_memory_space_constraint(array, pltpu.HBM)


def stack(values, extras=()):
    rows, half = values[0].shape[-2:]
    blocks = sum(value.size for value in values) // (rows * half)
    return pl.pallas_call(
        functools.partial(stack_kernel, len(values)),
        in_specs=[VMEM] * (len(values) + len(extras)),
        out_specs=VMEM,
        out_shape=jax.ShapeDtypeStruct((blocks, rows, half), values[0].dtype),
        compiler_params=pltpu.CompilerParams(vmem_limit_bytes=2 << 20),
    )(*values, *extras)


def near(array):
    return pltpu.with_memory_space_constraint(array, pltpu.VMEM)


def swap_devices(value, offset, devices):
    return lax.ppermute(value, "devs", [(d, d ^ offset) for d in range(devices)])


def swap_cores(value):
    return lax.ppermute(value, "pair", [(0, 1), (1, 0)])


def on_device(
    query, key_cache, value_cache, lengths, residual, router, routes, w_gate, w_up, w_down
):
    devices = lax.axis_size("devs")
    experts = router.shape[1]
    batches, per_batch, half = query.shape
    rows = batches * per_batch
    inputs = (
        query,
        key_cache,
        value_cache,
        lengths,
        residual,
        jnp.transpose(router),
        jnp.transpose(routes, (0, 2, 1)),
    )
    width, units = w_gate.shape
    block = min(512, units)
    piece = min(512, half)
    count = devices * rows
    owners = devices // experts
    hidden, meta = pl.pallas_call(
        attend_kernel,
        in_specs=[HBM] * 8,
        out_specs=[VMEM] * 2,
        out_shape=[
            jax.ShapeDtypeStruct((rows, half), jnp.bfloat16),
            jax.ShapeDtypeStruct((rows, LANES), jnp.float32),
        ],
        scratch_shapes=[
            (pltpu.SMEM if array.dtype == jnp.int32 else pltpu.VMEM)(array.shape, array.dtype)
            for array in inputs
        ]
        + [pltpu.VMEM((16, units), w_up.dtype), pltpu.SemaphoreType.DMA((8,))],
        compiler_params=pltpu.CompilerParams(vmem_limit_bytes=6 << 20),
    )(*[far(array) for array in inputs], far(w_up))

    offsets, near_rows, step = [0], hidden, 1
    while step < owners:
        arrived = swap_devices(near_rows, step, devices)
        extras = ()
        if step == 1:
            w_gate, w_up, w_down = near(w_gate), near(w_up), near(w_down)
            extras = (meta, w_gate)
        near_rows = stack((near_rows, arrived), extras)
        offsets += [offset ^ step for offset in offsets]
        step *= 2
    crossed = stack(
        [swap_devices(near_rows, k * owners, devices) for k in range(1, experts)],
        (w_up,),
    )
    offsets = [k * owners ^ offset for k in range(experts) for offset in offsets]
    others = [swap_cores(near_rows)]
    meta_other = swap_cores(meta)
    crossed, meta_other, others[0] = lax.optimization_barrier((crossed, meta_other, others[0]))
    others.append(swap_cores(crossed))
    held = [near_rows, crossed]
    parts = len(held)
    gates = pl.pallas_call(
        functools.partial(gate_kernel, block),
        in_specs=[VMEM] * (parts + 1),
        out_specs=VMEM,
        out_shape=jax.ShapeDtypeStruct((count, units), jnp.float32),
        compiler_params=pltpu.CompilerParams(vmem_limit_bytes=min(48, count // 16) << 20),
        cost_estimate=pl.CostEstimate(
            flops=2 * count * half * units, bytes_accessed=2 * half * units, transcendentals=0
        ),
    )(*held, w_gate)
    units_bf, weights = pl.pallas_call(
        functools.partial(expert_kernel, block, experts, parts),
        in_specs=[VMEM] * (2 * parts + 5),
        out_specs=[VMEM] * 2,
        out_shape=[
            jax.ShapeDtypeStruct((count, units), jnp.bfloat16),
            jax.ShapeDtypeStruct(meta.shape, jnp.float32),
        ],
        scratch_shapes=[pltpu.VMEM((count, width), jnp.bfloat16)],
        compiler_params=pltpu.CompilerParams(vmem_limit_bytes=min(48, count // 8) << 20),
    )(*held, *others, w_up, w_gate, gates, meta, meta_other)

    def project(own, dtype):
        return pl.pallas_call(
            functools.partial(down_kernel, piece, offsets, own),
            in_specs=[VMEM] * 2,
            out_specs=VMEM,
            out_shape=jax.ShapeDtypeStruct((devices, rows, half), dtype),
            compiler_params=pltpu.CompilerParams(vmem_limit_bytes=min(48, count // 16) << 20),
            cost_estimate=pl.CostEstimate(
                flops=2 * count * half * units,
                bytes_accessed=2 * half * units,
                transcendentals=0,
            ),
        )(units_bf, w_down)

    received = swap_cores(project(False, jnp.bfloat16))
    kept = project(True, jnp.float32)
    summed = pl.pallas_call(
        add_kernel,
        in_specs=[VMEM] * 2,
        out_specs=VMEM,
        out_shape=jax.ShapeDtypeStruct((devices, rows, half), jnp.bfloat16),
        compiler_params=pltpu.CompilerParams(vmem_limit_bytes=min(48, count // 16) << 20),
    )(kept, received)
    returned = lax.all_to_all(summed, "devs", split_axis=0, concat_axis=0, tiled=True)
    return pl.pallas_call(
        functools.partial(combine_kernel, experts),
        in_specs=[VMEM] * 3,
        out_specs=VMEM,
        out_shape=jax.ShapeDtypeStruct(query.shape, jnp.bfloat16),
        compiler_params=pltpu.CompilerParams(vmem_limit_bytes=6 << 20),
    )(returned, hidden, weights)


def solution(mesh):
    in_specs = (
        P(None, ("groups", "devs"), "pair"),
        P(None, ("groups", "devs"), None, "pair"),
        P(None, ("groups", "devs"), None, "pair"),
        P(None, ("groups", "devs")),
        P(None, ("groups", "devs"), "pair"),
        P("pair", None),
        P(None, ("groups", "devs"), None),
        P(None, ("devs", "pair")),
        P(None, ("devs", "pair")),
        P(("devs", "pair"), None),
    )
    out_specs = P(None, ("groups", "devs"), "pair")
    return jax.shard_map(
        on_device, mesh=mesh, in_specs=in_specs, out_specs=out_specs, check_vma=False
    )
```

```python
import functools
import math

import jax
import jax.numpy as jnp
from jax import lax
from jax.experimental import pallas as pl
from jax.experimental.pallas import tpu as pltpu
from jax.sharding import PartitionSpec as P

HD = 128
LANES = 128


def attend_kernel(
    query_hbm,
    key_hbm,
    value_hbm,
    lengths_hbm,
    residual_hbm,
    router_hbm,
    routes_hbm,
    up_hbm,
    hidden_ref,
    meta_ref,
    query_ref,
    key_ref,
    value_ref,
    lengths_ref,
    residual_ref,
    router_ref,
    routes_ref,
    up_ref,
    arrival,
):
    batches, per_batch, width = query_ref.shape
    rows = batches * per_batch
    cache_len = key_ref.shape[2]
    kv_local = key_ref.shape[3] // HD
    group = width // key_ref.shape[3]
    early = [(query_hbm, query_ref), (lengths_hbm, lengths_ref), (key_hbm, key_ref)]
    late = [
        (value_hbm, value_ref),
        (residual_hbm, residual_ref),
        (router_hbm, router_ref),
        (routes_hbm, routes_ref),
        (up_hbm.at[pl.ds(0, up_ref.shape[0])], up_ref),
    ]
    copies = [
        pltpu.make_async_copy(source, target, arrival.at[i])
        for i, (source, target) in enumerate(early + late)
    ]
    for copy in copies:
        copy.start()
    for copy in copies[: len(early)]:
        copy.wait()

    def stacked(ref):
        return jnp.concatenate([ref[b].astype(jnp.float32) for b in range(batches)], axis=0)

    queries = stacked(query_ref)
    tall = group * rows
    row_of = lax.rem(lax.broadcasted_iota(jnp.int32, (tall, 1), 0), rows)
    position = lax.broadcasted_iota(jnp.int32, (tall, cache_len), 1)
    limit = jnp.zeros((tall, 1), jnp.int32)
    for r in range(rows):
        limit = jnp.where(row_of == r, lengths_ref[r // per_batch, r % per_batch], limit)
    live = position < limit
    pieces, all_scores = [], []
    for k in range(kv_local):
        heads = jnp.concatenate(
            [queries[:, (k * group + j) * HD : (k * group + j + 1) * HD] for j in range(group)],
            axis=0,
        ).astype(jnp.bfloat16)
        columns = slice(k * HD, (k + 1) * HD)
        scores = jnp.zeros((tall, cache_len), jnp.float32)
        for r in range(rows):
            keys = key_ref[r // per_batch, r % per_batch, :, columns]
            part = lax.dot_general(
                heads, keys, (((1,), (1,)), ((), ())), preferred_element_type=jnp.float32
            )
            scores = jnp.where(row_of == r, part, scores)
        all_scores.append(scores)
    for copy in copies[len(early) :]:
        copy.wait()
    for k, scores in enumerate(all_scores):
        columns = slice(k * HD, (k + 1) * HD)
        scores = jnp.where(live, scores * (1.0 / math.sqrt(HD)), -jnp.inf)
        peak = jnp.max(scores, axis=-1, keepdims=True)
        weights = jnp.where(live, jnp.exp(scores - peak), 0.0)
        total = jnp.sum(weights, axis=-1, keepdims=True)
        weights_bf = weights.astype(jnp.bfloat16)
        mixed = jnp.zeros((tall, HD), jnp.float32)
        for r in range(rows):
            values = value_ref[r // per_batch, r % per_batch, :, columns]
            part = jnp.dot(weights_bf, values, preferred_element_type=jnp.float32)
            mixed = jnp.where(row_of == r, part, mixed)
        mixed = mixed / total
        pieces += [mixed[j * rows : (j + 1) * rows] for j in range(group)]
    attended = jnp.concatenate(pieces, axis=1)
    hidden = (stacked(residual_ref) + attended).astype(jnp.bfloat16)
    wide = hidden.astype(jnp.float32)
    logits = lax.dot_general(
        hidden, router_ref[...], (((1,), (1,)), ((), ())), preferred_element_type=jnp.float32
    )
    squares = jnp.sum(wide * wide, axis=-1, keepdims=True)
    experts = router_ref.shape[0]
    row = lax.broadcasted_iota(jnp.int32, (rows, 1), 0)
    meta_ref[...] = jnp.zeros_like(meta_ref)
    meta_ref[:, :experts] = logits
    meta_ref[:, experts : experts + 1] = squares
    for which in range(2):
        route = jnp.zeros((rows, 1), jnp.int32)
        for r in range(rows):
            route = jnp.where(row == r, routes_ref[r // per_batch, which, r % per_batch], route)
        lane = experts + 1 + which
        meta_ref[:, lane : lane + 1] = route.astype(jnp.float32)
    hidden_ref[...] = hidden


def stack_kernel(count, *refs):
    out_ref, start = refs[-1], 0
    for ref in refs[:count]:
        if ref.ndim == 2:
            out_ref[start] = ref[...]
            start += 1
        else:
            out_ref[start : start + ref.shape[0]] = ref[...]
            start += ref.shape[0]


def rows_of(refs):
    half = refs[0].shape[-1]
    tall = [ref[...].astype(jnp.float32).reshape(-1, half) for ref in refs]
    return jnp.concatenate(tall, axis=0)


def half_starts(half):
    side = lax.axis_index("pair")
    return (
        pl.multiple_of(side * half, LANES),
        pl.multiple_of((1 - side) * half, LANES),
    )


def gate_kernel(block, *refs):
    *own_refs, gate_ref, gates_ref = refs
    half = own_refs[0].shape[-1]
    units = gate_ref.shape[1]
    own_start, _ = half_starts(half)
    rows = rows_of(own_refs).astype(jnp.bfloat16)
    for start in range(0, units, block):
        part = slice(start, start + block)
        gates_ref[:, part] = jnp.dot(
            rows, gate_ref[pl.ds(own_start, half), part], preferred_element_type=jnp.float32
        )


def store_rows(target, columns, product):
    blocks, rows, _ = target.shape
    for j in range(blocks):
        target[j, :, columns] = product[j * rows : (j + 1) * rows].astype(target.dtype)


def expert_kernel(block, experts, parts, *refs):
    own_refs, refs = refs[:parts], refs[parts:]
    other_refs, refs = refs[:parts], refs[parts:]
    (
        up_ref,
        gate_ref,
        gates_ref,
        meta_ref,
        meta_other_ref,
        units_ref,
        weights_ref,
        rows_ref,
    ) = refs
    width = rows_ref.shape[1]
    half = width // 2
    units = gate_ref.shape[1]
    own_start, other_start = half_starts(half)

    own, other = rows_of(own_refs), rows_of(other_refs)
    squares = jnp.sum(own * own, axis=-1, keepdims=True) + jnp.sum(
        other * other, axis=-1, keepdims=True
    )
    inv_rms = lax.rsqrt(squares / width + 1e-05)
    other = other.astype(jnp.bfloat16)
    rows_ref[:, pl.ds(own_start, half)] = own.astype(jnp.bfloat16)
    rows_ref[:, pl.ds(other_start, half)] = other

    for start in range(0, units, block):
        part = slice(start, start + block)
        gate = gates_ref[:, part] + jnp.dot(
            other, gate_ref[pl.ds(other_start, half), part], preferred_element_type=jnp.float32
        )
        gate = jax.nn.silu(gate * inv_rms) * inv_rms
        up = jnp.dot(rows_ref[...], up_ref[:, part], preferred_element_type=jnp.float32)
        units_ref[:, part] = (gate * up).astype(jnp.bfloat16)

    meta = meta_ref[...] + meta_other_ref[...]
    logits = meta * lax.rsqrt(meta[:, experts : experts + 1] / width + 1e-05)
    chosen = meta_ref[:, experts + 1 : experts + 3].astype(jnp.int32)
    first, second = chosen[:, 0:1], chosen[:, 1:2]
    lane = lax.broadcasted_iota(jnp.int32, meta.shape, 1)
    logit_first = jnp.sum(jnp.where(lane == first, logits, 0.0), axis=-1, keepdims=True)
    logit_second = jnp.sum(jnp.where(lane == second, logits, 0.0), axis=-1, keepdims=True)
    weights_ref[...] = jnp.where(
        lane == first, jax.nn.sigmoid(logit_first - logit_second), 0.0
    ) + jnp.where(lane == second, jax.nn.sigmoid(logit_second - logit_first), 0.0)


def down_kernel(piece, own, units_ref, down_ref, out_ref):
    half = out_ref.shape[-1]
    base = half_starts(half)[0 if own else 1]
    for start in range(0, half, piece):
        columns = pl.ds(pl.multiple_of(base + start, LANES), piece)
        product = jnp.dot(
            units_ref[...], down_ref[:, columns], preferred_element_type=jnp.float32
        )
        store_rows(out_ref, slice(start, start + piece), product)


def add_kernel(kept_ref, received_ref, near_ref, *far_refs):
    total = kept_ref[...] + received_ref[...].astype(jnp.float32)
    size = near_ref.shape[0]
    near_ref[...] = total[:size]
    for i, ref in enumerate(far_refs):
        start = size + i * ref.shape[0]
        ref[...] = total[start : start + ref.shape[0]].astype(jnp.bfloat16)


def mix_kernel(owners, weights_ref, *refs):
    *expert_refs, kept_ref, sent_ref = refs
    home = lax.axis_index("devs") // owners
    lane = lax.broadcasted_iota(jnp.int32, weights_ref.shape[1:], 1)
    for block in range(owners):
        weights = weights_ref[block]
        total = None
        for k, ref in enumerate(expert_refs):
            mine = lane == lax.bitwise_xor(home, k)
            weight = jnp.sum(jnp.where(mine, weights, 0.0), axis=-1, keepdims=True)
            product = weight * ref[block].astype(jnp.float32)
            total = product if total is None else total + product
        kept = kept_ref.shape[0]
        if block < kept:
            kept_ref[block] = total
        else:
            sent_ref[block - kept] = total.astype(jnp.bfloat16)


def finish_kernel(hidden_ref, kept_ref, received_ref, out_ref):
    batches, per_batch, _ = out_ref.shape
    result = (
        hidden_ref[...].astype(jnp.float32)
        + kept_ref[0]
        + received_ref[0].astype(jnp.float32)
    )
    for b in range(batches):
        out_ref[b] = result[b * per_batch : (b + 1) * per_batch].astype(jnp.bfloat16)


VMEM = pl.BlockSpec(memory_space=pltpu.VMEM)
HBM = pl.BlockSpec(memory_space=pltpu.HBM)


def far(array):
    return pltpu.with_memory_space_constraint(array, pltpu.HBM)


def stack(values, extras=()):
    rows, half = values[0].shape[-2:]
    blocks = sum(value.size for value in values) // (rows * half)
    return pl.pallas_call(
        functools.partial(stack_kernel, len(values)),
        in_specs=[VMEM] * (len(values) + len(extras)),
        out_specs=VMEM,
        out_shape=jax.ShapeDtypeStruct((blocks, rows, half), values[0].dtype),
        compiler_params=pltpu.CompilerParams(vmem_limit_bytes=2 << 20),
    )(*values, *extras)


def add(kept, received, count):
    blocks, rows, half = kept.shape
    size = blocks // (count + 1)
    return pl.pallas_call(
        add_kernel,
        in_specs=[VMEM] * 2,
        out_specs=[VMEM] * (count + 1),
        out_shape=[jax.ShapeDtypeStruct((size, rows, half), jnp.float32)]
        + [jax.ShapeDtypeStruct((size, rows, half), jnp.bfloat16)] * count,
        compiler_params=pltpu.CompilerParams(vmem_limit_bytes=min(48, max(4, blocks // 2)) << 20),
    )(kept, received)


def near(array):
    return pltpu.with_memory_space_constraint(array, pltpu.VMEM)


def swap_devices(value, offset, devices):
    return lax.ppermute(value, "devs", [(d, d ^ offset) for d in range(devices)])


def swap_cores(value):
    return lax.ppermute(value, "pair", [(0, 1), (1, 0)])


def on_device(
    query, key_cache, value_cache, lengths, residual, router, routes, w_gate, w_up, w_down
):
    devices = lax.axis_size("devs")
    experts = router.shape[1]
    batches, per_batch, half = query.shape
    rows = batches * per_batch
    inputs = (
        query,
        key_cache,
        value_cache,
        lengths,
        residual,
        jnp.transpose(router),
        jnp.transpose(routes, (0, 2, 1)),
    )
    width, units = w_gate.shape
    block = min(512, units)
    piece = min(512, half)
    count = devices * rows
    owners = devices // experts
    hidden, meta = pl.pallas_call(
        attend_kernel,
        in_specs=[HBM] * 8,
        out_specs=[VMEM] * 2,
        out_shape=[
            jax.ShapeDtypeStruct((rows, half), jnp.bfloat16),
            jax.ShapeDtypeStruct((rows, LANES), jnp.float32),
        ],
        scratch_shapes=[
            (pltpu.SMEM if array.dtype == jnp.int32 else pltpu.VMEM)(array.shape, array.dtype)
            for array in inputs
        ]
        + [pltpu.VMEM((16, units), w_up.dtype), pltpu.SemaphoreType.DMA((8,))],
        compiler_params=pltpu.CompilerParams(vmem_limit_bytes=6 << 20),
    )(*[far(array) for array in inputs], far(w_up))

    offsets, near_rows, step = [0], hidden, 1
    while step < owners:
        arrived = swap_devices(near_rows, step, devices)
        extras = ()
        if step == 1:
            w_gate, w_up, w_down = near(w_gate), near(w_up), near(w_down)
            extras = (meta, w_gate)
        near_rows = stack((near_rows, arrived), extras)
        offsets += [offset ^ step for offset in offsets]
        step *= 2
    crossed = stack(
        [swap_devices(near_rows, k * owners, devices) for k in range(1, experts)],
        (w_up,),
    )
    offsets = [k * owners ^ offset for k in range(experts) for offset in offsets]
    others = [swap_cores(near_rows)]
    meta_other = swap_cores(meta)
    crossed, meta_other, others[0] = lax.optimization_barrier((crossed, meta_other, others[0]))
    others.append(swap_cores(crossed))
    held = [near_rows, crossed]
    parts = len(held)
    gates = pl.pallas_call(
        functools.partial(gate_kernel, block),
        in_specs=[VMEM] * (parts + 1),
        out_specs=VMEM,
        out_shape=jax.ShapeDtypeStruct((count, units), jnp.float32),
        compiler_params=pltpu.CompilerParams(vmem_limit_bytes=min(48, count // 16) << 20),
        cost_estimate=pl.CostEstimate(
            flops=2 * count * half * units, bytes_accessed=2 * half * units, transcendentals=0
        ),
    )(*held, w_gate)
    units_bf, weights = pl.pallas_call(
        functools.partial(expert_kernel, block, experts, parts),
        in_specs=[VMEM] * (2 * parts + 5),
        out_specs=[VMEM] * 2,
        out_shape=[
            jax.ShapeDtypeStruct((count, units), jnp.bfloat16),
            jax.ShapeDtypeStruct(meta.shape, jnp.float32),
        ],
        scratch_shapes=[pltpu.VMEM((count, width), jnp.bfloat16)],
        compiler_params=pltpu.CompilerParams(vmem_limit_bytes=min(48, count // 8) << 20),
    )(*held, *others, w_up, w_gate, gates, meta, meta_other)

    def project(own, dtype):
        return pl.pallas_call(
            functools.partial(down_kernel, piece, own),
            in_specs=[VMEM] * 2,
            out_specs=VMEM,
            out_shape=jax.ShapeDtypeStruct((devices, rows, half), dtype),
            compiler_params=pltpu.CompilerParams(vmem_limit_bytes=min(48, count // 16) << 20),
            cost_estimate=pl.CostEstimate(
                flops=2 * count * half * units,
                bytes_accessed=2 * half * units,
                transcendentals=0,
            ),
        )(units_bf, w_down)

    received = swap_cores(project(False, jnp.bfloat16))
    kept = project(True, jnp.float32)
    kept, *sent = add(kept, received, experts - 1)
    returned = [
        swap_devices(value, k * owners, devices) for k, value in enumerate(sent, 1)
    ]
    weights_all, reach = weights, 1
    while reach < owners:
        weights_all = stack((weights_all, swap_devices(weights_all, reach, devices)))
        reach *= 2
    step = owners // 2
    kept, sent = pl.pallas_call(
        functools.partial(mix_kernel, owners),
        in_specs=[VMEM] * (experts + 1),
        out_specs=[VMEM] * 2,
        out_shape=[
            jax.ShapeDtypeStruct((step, rows, half), jnp.float32),
            jax.ShapeDtypeStruct((step, rows, half), jnp.bfloat16),
        ],
        compiler_params=pltpu.CompilerParams(vmem_limit_bytes=min(48, max(4, owners)) << 20),
    )(weights_all, kept, *returned)
    received = swap_devices(sent, step, devices)
    while step > 1:
        step //= 2
        kept, sent = add(kept, received, 1)
        received = swap_devices(sent, step, devices)
    return pl.pallas_call(
        finish_kernel,
        in_specs=[VMEM] * 3,
        out_specs=VMEM,
        out_shape=jax.ShapeDtypeStruct(query.shape, jnp.bfloat16),
        compiler_params=pltpu.CompilerParams(vmem_limit_bytes=4 << 20),
    )(hidden, kept, received)


def solution(mesh):
    in_specs = (
        P(None, ("groups", "devs"), "pair"),
        P(None, ("groups", "devs"), None, "pair"),
        P(None, ("groups", "devs"), None, "pair"),
        P(None, ("groups", "devs")),
        P(None, ("groups", "devs"), "pair"),
        P("pair", None),
        P(None, ("groups", "devs"), None),
        P(None, ("devs", "pair")),
        P(None, ("devs", "pair")),
        P(("devs", "pair"), None),
    )
    out_specs = P(None, ("groups", "devs"), "pair")
    return jax.shard_map(
        on_device, mesh=mesh, in_specs=in_specs, out_specs=out_specs, check_vma=False
    )
```

```python
import functools
import math

import jax
import jax.numpy as jnp
from jax import lax
from jax.experimental import pallas as pl
from jax.experimental.pallas import tpu as pltpu
from jax.sharding import PartitionSpec as P

HD = 128
LANES = 128


def attend_kernel(
    query_hbm,
    key_hbm,
    value_hbm,
    lengths_hbm,
    residual_hbm,
    router_hbm,
    routes_hbm,
    up_hbm,
    hidden_ref,
    meta_ref,
    query_ref,
    key_ref,
    value_ref,
    lengths_ref,
    residual_ref,
    router_ref,
    routes_ref,
    up_ref,
    arrival,
):
    batches, per_batch, width = query_ref.shape
    rows = batches * per_batch
    cache_len = key_ref.shape[2]
    kv_local = key_ref.shape[3] // HD
    group = width // key_ref.shape[3]
    early = [(query_hbm, query_ref), (lengths_hbm, lengths_ref)]
    early += [(key_hbm.at[b], key_ref.at[b]) for b in range(batches)]
    late = [
        (value_hbm, value_ref),
        (residual_hbm, residual_ref),
        (router_hbm, router_ref),
        (routes_hbm, routes_ref),
        (up_hbm.at[pl.ds(0, up_ref.shape[0])], up_ref),
    ]
    copies = [
        pltpu.make_async_copy(source, target, arrival.at[i])
        for i, (source, target) in enumerate(early + late)
    ]
    for copy in copies:
        copy.start()
    for copy in copies[:2]:
        copy.wait()

    def stacked(ref):
        return jnp.concatenate([ref[b].astype(jnp.float32) for b in range(batches)], axis=0)

    queries = stacked(query_ref)
    tall = group * rows
    row_of = lax.rem(lax.broadcasted_iota(jnp.int32, (tall, 1), 0), rows)
    position = lax.broadcasted_iota(jnp.int32, (tall, cache_len), 1)
    limit = jnp.zeros((tall, 1), jnp.int32)
    for r in range(rows):
        limit = jnp.where(row_of == r, lengths_ref[r // per_batch, r % per_batch], limit)
    live = position < limit
    pieces, all_heads = [], []
    for k in range(kv_local):
        heads = jnp.concatenate(
            [queries[:, (k * group + j) * HD : (k * group + j + 1) * HD] for j in range(group)],
            axis=0,
        )
        all_heads.append(heads.astype(jnp.bfloat16))
    all_scores = [jnp.zeros((tall, cache_len), jnp.float32)] * kv_local
    for b in range(batches):
        copies[2 + b].wait()
        for k in range(kv_local):
            columns = slice(k * HD, (k + 1) * HD)
            for r in range(b * per_batch, (b + 1) * per_batch):
                keys = key_ref[b, r % per_batch, :, columns]
                part = lax.dot_general(
                    all_heads[k],
                    keys,
                    (((1,), (1,)), ((), ())),
                    preferred_element_type=jnp.float32,
                )
                all_scores[k] = jnp.where(row_of == r, part, all_scores[k])
    for copy in copies[len(early) :]:
        copy.wait()
    for k, scores in enumerate(all_scores):
        columns = slice(k * HD, (k + 1) * HD)
        scores = jnp.where(live, scores * (1.0 / math.sqrt(HD)), -jnp.inf)
        peak = jnp.max(scores, axis=-1, keepdims=True)
        weights = jnp.where(live, jnp.exp(scores - peak), 0.0)
        total = jnp.sum(weights, axis=-1, keepdims=True)
        weights_bf = weights.astype(jnp.bfloat16)
        mixed = jnp.zeros((tall, HD), jnp.float32)
        for r in range(rows):
            values = value_ref[r // per_batch, r % per_batch, :, columns]
            part = jnp.dot(weights_bf, values, preferred_element_type=jnp.float32)
            mixed = jnp.where(row_of == r, part, mixed)
        mixed = mixed / total
        pieces += [mixed[j * rows : (j + 1) * rows] for j in range(group)]
    attended = jnp.concatenate(pieces, axis=1)
    hidden = (stacked(residual_ref) + attended).astype(jnp.bfloat16)
    wide = hidden.astype(jnp.float32)
    logits = lax.dot_general(
        hidden, router_ref[...], (((1,), (1,)), ((), ())), preferred_element_type=jnp.float32
    )
    squares = jnp.sum(wide * wide, axis=-1, keepdims=True)
    experts = router_ref.shape[0]
    row = lax.broadcasted_iota(jnp.int32, (rows, 1), 0)
    meta_ref[...] = jnp.zeros_like(meta_ref)
    meta_ref[:, :experts] = logits
    meta_ref[:, experts : experts + 1] = squares
    for which in range(2):
        route = jnp.zeros((rows, 1), jnp.int32)
        for r in range(rows):
            route = jnp.where(row == r, routes_ref[r // per_batch, which, r % per_batch], route)
        lane = experts + 1 + which
        meta_ref[:, lane : lane + 1] = route.astype(jnp.float32)
    hidden_ref[...] = hidden


def stack_kernel(count, *refs):
    out_ref, start = refs[-1], 0
    for ref in refs[:count]:
        if ref.ndim == 2:
            out_ref[start] = ref[...]
            start += 1
        else:
            out_ref[start : start + ref.shape[0]] = ref[...]
            start += ref.shape[0]


def rows_of(refs):
    half = refs[0].shape[-1]
    tall = [ref[...].astype(jnp.float32).reshape(-1, half) for ref in refs]
    return jnp.concatenate(tall, axis=0)


def half_starts(half):
    side = lax.axis_index("pair")
    return (
        pl.multiple_of(side * half, LANES),
        pl.multiple_of((1 - side) * half, LANES),
    )


def gate_kernel(block, *refs):
    *own_refs, gate_ref, gates_ref = refs
    half = own_refs[0].shape[-1]
    units = gate_ref.shape[1]
    own_start, _ = half_starts(half)
    rows = rows_of(own_refs).astype(jnp.bfloat16)
    for start in range(0, units, block):
        part = slice(start, start + block)
        gates_ref[:, part] = jnp.dot(
            rows, gate_ref[pl.ds(own_start, half), part], preferred_element_type=jnp.float32
        )


def store_rows(target, columns, product):
    blocks, rows, _ = target.shape
    for j in range(blocks):
        target[j, :, columns] = product[j * rows : (j + 1) * rows].astype(target.dtype)


def expert_kernel(block, experts, parts, *refs):
    own_refs, refs = refs[:parts], refs[parts:]
    other_refs, refs = refs[:parts], refs[parts:]
    (
        up_ref,
        gate_ref,
        gates_ref,
        meta_ref,
        meta_other_ref,
        units_ref,
        weights_ref,
        rows_ref,
    ) = refs
    width = rows_ref.shape[1]
    half = width // 2
    units = gate_ref.shape[1]
    own_start, other_start = half_starts(half)

    own, other = rows_of(own_refs), rows_of(other_refs)
    squares = jnp.sum(own * own, axis=-1, keepdims=True) + jnp.sum(
        other * other, axis=-1, keepdims=True
    )
    inv_rms = lax.rsqrt(squares / width + 1e-05)
    other = other.astype(jnp.bfloat16)
    rows_ref[:, pl.ds(own_start, half)] = own.astype(jnp.bfloat16)
    rows_ref[:, pl.ds(other_start, half)] = other

    for start in range(0, units, block):
        part = slice(start, start + block)
        gate = gates_ref[:, part] + jnp.dot(
            other, gate_ref[pl.ds(other_start, half), part], preferred_element_type=jnp.float32
        )
        gate = jax.nn.silu(gate * inv_rms) * inv_rms
        up = jnp.dot(rows_ref[...], up_ref[:, part], preferred_element_type=jnp.float32)
        units_ref[:, part] = (gate * up).astype(jnp.bfloat16)

    meta = meta_ref[...] + meta_other_ref[...]
    logits = meta * lax.rsqrt(meta[:, experts : experts + 1] / width + 1e-05)
    chosen = meta_ref[:, experts + 1 : experts + 3].astype(jnp.int32)
    first, second = chosen[:, 0:1], chosen[:, 1:2]
    lane = lax.broadcasted_iota(jnp.int32, meta.shape, 1)
    logit_first = jnp.sum(jnp.where(lane == first, logits, 0.0), axis=-1, keepdims=True)
    logit_second = jnp.sum(jnp.where(lane == second, logits, 0.0), axis=-1, keepdims=True)
    weights_ref[...] = jnp.where(
        lane == first, jax.nn.sigmoid(logit_first - logit_second), 0.0
    ) + jnp.where(lane == second, jax.nn.sigmoid(logit_second - logit_first), 0.0)


def down_kernel(piece, own, units_ref, down_ref, out_ref):
    half = out_ref.shape[-1]
    base = half_starts(half)[0 if own else 1]
    for start in range(0, half, piece):
        columns = pl.ds(pl.multiple_of(base + start, LANES), piece)
        product = jnp.dot(
            units_ref[...], down_ref[:, columns], preferred_element_type=jnp.float32
        )
        store_rows(out_ref, slice(start, start + piece), product)


def add_kernel(kept_ref, received_ref, near_ref, *far_refs):
    total = kept_ref[...] + received_ref[...].astype(jnp.float32)
    size = near_ref.shape[0]
    near_ref[...] = total[:size]
    for i, ref in enumerate(far_refs):
        start = size + i * ref.shape[0]
        ref[...] = total[start : start + ref.shape[0]].astype(jnp.bfloat16)


def mix_kernel(owners, weights_ref, *refs):
    *expert_refs, kept_ref, sent_ref = refs
    home = lax.axis_index("devs") // owners
    lane = lax.broadcasted_iota(jnp.int32, weights_ref.shape[1:], 1)
    for block in range(owners):
        weights = weights_ref[block]
        total = None
        for k, ref in enumerate(expert_refs):
            mine = lane == lax.bitwise_xor(home, k)
            weight = jnp.sum(jnp.where(mine, weights, 0.0), axis=-1, keepdims=True)
            product = weight * ref[block].astype(jnp.float32)
            total = product if total is None else total + product
        kept = kept_ref.shape[0]
        if block < kept:
            kept_ref[block] = total
        else:
            sent_ref[block - kept] = total.astype(jnp.bfloat16)


def finish_kernel(hidden_ref, kept_ref, received_ref, out_ref):
    batches, per_batch, _ = out_ref.shape
    result = (
        hidden_ref[...].astype(jnp.float32)
        + kept_ref[0]
        + received_ref[0].astype(jnp.float32)
    )
    for b in range(batches):
        out_ref[b] = result[b * per_batch : (b + 1) * per_batch].astype(jnp.bfloat16)


VMEM = pl.BlockSpec(memory_space=pltpu.VMEM)
HBM = pl.BlockSpec(memory_space=pltpu.HBM)


def far(array):
    return pltpu.with_memory_space_constraint(array, pltpu.HBM)


def stack(values, extras=()):
    rows, half = values[0].shape[-2:]
    blocks = sum(value.size for value in values) // (rows * half)
    return pl.pallas_call(
        functools.partial(stack_kernel, len(values)),
        in_specs=[VMEM] * (len(values) + len(extras)),
        out_specs=VMEM,
        out_shape=jax.ShapeDtypeStruct((blocks, rows, half), values[0].dtype),
        compiler_params=pltpu.CompilerParams(vmem_limit_bytes=2 << 20),
    )(*values, *extras)


def add(kept, received, count):
    blocks, rows, half = kept.shape
    size = blocks // (count + 1)
    return pl.pallas_call(
        add_kernel,
        in_specs=[VMEM] * 2,
        out_specs=[VMEM] * (count + 1),
        out_shape=[jax.ShapeDtypeStruct((size, rows, half), jnp.float32)]
        + [jax.ShapeDtypeStruct((size, rows, half), jnp.bfloat16)] * count,
        compiler_params=pltpu.CompilerParams(vmem_limit_bytes=min(48, max(4, blocks // 2)) << 20),
    )(kept, received)


def near(array):
    return pltpu.with_memory_space_constraint(array, pltpu.VMEM)


def swap_devices(value, offset, devices):
    return lax.ppermute(value, "devs", [(d, d ^ offset) for d in range(devices)])


def swap_cores(value):
    return lax.ppermute(value, "pair", [(0, 1), (1, 0)])


def on_device(
    query, key_cache, value_cache, lengths, residual, router, routes, w_gate, w_up, w_down
):
    devices = lax.axis_size("devs")
    experts = router.shape[1]
    batches, per_batch, half = query.shape
    rows = batches * per_batch
    inputs = (
        query,
        key_cache,
        value_cache,
        lengths,
        residual,
        jnp.transpose(router),
        jnp.transpose(routes, (0, 2, 1)),
    )
    width, units = w_gate.shape
    block = min(512, units)
    piece = min(768, half)
    count = devices * rows
    owners = devices // experts
    hidden, meta = pl.pallas_call(
        attend_kernel,
        in_specs=[HBM] * 8,
        out_specs=[VMEM] * 2,
        out_shape=[
            jax.ShapeDtypeStruct((rows, half), jnp.bfloat16),
            jax.ShapeDtypeStruct((rows, LANES), jnp.float32),
        ],
        scratch_shapes=[
            (pltpu.SMEM if array.dtype == jnp.int32 else pltpu.VMEM)(array.shape, array.dtype)
            for array in inputs
        ]
        + [pltpu.VMEM((16, units), w_up.dtype), pltpu.SemaphoreType.DMA((7 + batches,))],
        compiler_params=pltpu.CompilerParams(vmem_limit_bytes=6 << 20),
    )(*[far(array) for array in inputs], far(w_up))

    offsets, near_rows, step = [0], hidden, 1
    while step < owners:
        arrived = swap_devices(near_rows, step, devices)
        extras = ()
        if step == 1:
            w_gate, w_up, w_down = near(w_gate), near(w_up), near(w_down)
            extras = (meta, w_gate)
        near_rows = stack((near_rows, arrived), extras)
        offsets += [offset ^ step for offset in offsets]
        step *= 2
    crossed = stack(
        [swap_devices(near_rows, k * owners, devices) for k in range(1, experts)],
        (w_up,),
    )
    offsets = [k * owners ^ offset for k in range(experts) for offset in offsets]
    others = [swap_cores(near_rows)]
    meta_other = swap_cores(meta)
    crossed, meta_other, others[0] = lax.optimization_barrier((crossed, meta_other, others[0]))
    others.append(swap_cores(crossed))
    held = [near_rows, crossed]
    parts = len(held)
    gates = pl.pallas_call(
        functools.partial(gate_kernel, block),
        in_specs=[VMEM] * (parts + 1),
        out_specs=VMEM,
        out_shape=jax.ShapeDtypeStruct((count, units), jnp.float32),
        compiler_params=pltpu.CompilerParams(vmem_limit_bytes=min(48, count // 16) << 20),
        cost_estimate=pl.CostEstimate(
            flops=2 * count * half * units, bytes_accessed=2 * half * units, transcendentals=0
        ),
    )(*held, w_gate)
    units_bf, weights = pl.pallas_call(
        functools.partial(expert_kernel, block, experts, parts),
        in_specs=[VMEM] * (2 * parts + 5),
        out_specs=[VMEM] * 2,
        out_shape=[
            jax.ShapeDtypeStruct((count, units), jnp.bfloat16),
            jax.ShapeDtypeStruct(meta.shape, jnp.float32),
        ],
        scratch_shapes=[pltpu.VMEM((count, width), jnp.bfloat16)],
        compiler_params=pltpu.CompilerParams(vmem_limit_bytes=min(48, count // 8) << 20),
    )(*held, *others, w_up, w_gate, gates, meta, meta_other)

    def project(own, dtype):
        return pl.pallas_call(
            functools.partial(down_kernel, piece, own),
            in_specs=[VMEM] * 2,
            out_specs=VMEM,
            out_shape=jax.ShapeDtypeStruct((devices, rows, half), dtype),
            compiler_params=pltpu.CompilerParams(vmem_limit_bytes=min(48, count // 16) << 20),
            cost_estimate=pl.CostEstimate(
                flops=2 * count * half * units,
                bytes_accessed=2 * half * units,
                transcendentals=0,
            ),
        )(units_bf, w_down)

    received = swap_cores(project(False, jnp.bfloat16))
    kept = project(True, jnp.float32)
    kept, *sent = add(kept, received, experts - 1)
    returned = [
        swap_devices(value, k * owners, devices) for k, value in enumerate(sent, 1)
    ]
    weights_all, reach = weights, 1
    while reach < owners:
        weights_all = stack((weights_all, swap_devices(weights_all, reach, devices)))
        reach *= 2
    step = owners // 2
    kept, sent = pl.pallas_call(
        functools.partial(mix_kernel, owners),
        in_specs=[VMEM] * (experts + 1),
        out_specs=[VMEM] * 2,
        out_shape=[
            jax.ShapeDtypeStruct((step, rows, half), jnp.float32),
            jax.ShapeDtypeStruct((step, rows, half), jnp.bfloat16),
        ],
        compiler_params=pltpu.CompilerParams(vmem_limit_bytes=min(48, max(4, owners)) << 20),
    )(weights_all, kept, *returned)
    received = swap_devices(sent, step, devices)
    while step > 1:
        step //= 2
        kept, sent = add(kept, received, 1)
        received = swap_devices(sent, step, devices)
    return pl.pallas_call(
        finish_kernel,
        in_specs=[VMEM] * 3,
        out_specs=VMEM,
        out_shape=jax.ShapeDtypeStruct(query.shape, jnp.bfloat16),
        compiler_params=pltpu.CompilerParams(vmem_limit_bytes=4 << 20),
    )(hidden, kept, received)


def solution(mesh):
    in_specs = (
        P(None, ("groups", "devs"), "pair"),
        P(None, ("groups", "devs"), None, "pair"),
        P(None, ("groups", "devs"), None, "pair"),
        P(None, ("groups", "devs")),
        P(None, ("groups", "devs"), "pair"),
        P("pair", None),
        P(None, ("groups", "devs"), None),
        P(None, ("devs", "pair")),
        P(None, ("devs", "pair")),
        P(("devs", "pair"), None),
    )
    out_specs = P(None, ("groups", "devs"), "pair")
    return jax.shard_map(
        on_device, mesh=mesh, in_specs=in_specs, out_specs=out_specs, check_vma=False
    )
```
